512 devices in a mesh: grp: 16 (over y, z_hi), mem: 32 (over z_lo, x, core).
Axes of the slice: x: 4, y: 4, z: 16 (z_hi: 4, z_lo: 4; z = z_hi * 4 + z_lo), core: 2. Of those that a mesh axis runs over, the one named last changes fastest.
Arguments:
- activations: bfloat16 [2, 65536, 512], P(None, ('grp', 'mem'))
- out_grads: bfloat16 [2, 65536, 512], P(None, ('grp', 'mem'))
- inverse_slots: float32 [2, 2, 8192, 512], P(None, None, ('grp', 'mem')), as said below
- gradient: float32 [2, 512, 512], replicated, may hold values from -6 to 6
- owners: int32 [2, 2], replicated, may hold values from 0 to 15
- counts: int32 [512], replicated, may hold values from 32 to 128, as said below
Outputs:
- factor_slots: float32 [2, 2, 8192, 512], P(None, None, ('grp', 'mem'))
- preconditioned: float32 [2, 512, 512], P(None, 'mem', 'grp')
The draws below stay inside these ranges and needn't reach their ends.
Inputs may be any that keep to these rules, and one draw needn't show every extreme that they name: `counts`: live tokens of a device; some device has all 128 live in every draw. `inverse_slots`: symmetric in every slot.
All inputs are finite; a program needn't handle non-finite values.
Results may differ from the reference program's by a relative error of at most 0.0003.
Values sent between devices are 32-bit elements; how exact they have to be, the bound alone decides.
A program may use at most 64 MiB of HBM per device.

```python
import jax
import jax.numpy as jnp
from jax import lax

BLK = 512
LAYERS = 2
TOK_DEV = 128
TOKENS = 65536
N_GRP = 16
N_MEM = 32


def mixed_rows(key, base):
    key_rows, key_cols = jax.random.split(key)
    mixed = base + 0.6 * jnp.roll(base, 1, axis=2) + 0.4 * jnp.roll(base, 37, axis=2)
    row_scale = jnp.exp(jax.random.uniform(key_rows, (LAYERS, TOKENS, 1), jnp.float32, 0.0, 2.3))
    col_scale = jnp.exp(jax.random.uniform(key_cols, (LAYERS, 1, BLK), jnp.float32, -1.15, 1.15))
    return (mixed / 1.3 * row_scale * col_scale * 0.3).astype(jnp.bfloat16)


def draw_side(key):
    key_base = jax.random.fold_in(key, 0)
    key_scale = jax.random.fold_in(key, 2)
    base = jax.random.normal(key_base, (LAYERS, TOKENS, BLK), jnp.float32)
    return mixed_rows(key_scale, base)


def side_diagonal(key, shared):
    key_common = jax.random.fold_in(key, 1)
    key_scale = jax.random.fold_in(key, 2)
    key_cols = jax.random.fold_in(key_scale, 1)
    col_scale = jnp.exp(jax.random.uniform(key_cols, (LAYERS, 1, BLK), jnp.float32, -1.15, 1.15))
    common = shared * jax.random.normal(key_common, (LAYERS, 1, BLK), jnp.float32)
    second = 1.52 / 1.69 + common * common
    return (0.09 * 21.5 * col_scale * col_scale * second + 0.1)[:, 0, :]


def count_values(key):
    key = jax.random.fold_in(key, 53)
    key_vals, key_top = jax.random.split(key)
    values = jax.random.randint(key_vals, (N_GRP * N_MEM,), TOK_DEV // 4, TOK_DEV + 1)
    fullest = jax.random.randint(key_top, (), 0, N_GRP * N_MEM)
    return values.at[fullest].set(TOK_DEV).astype(jnp.int32)


def draw_activations(key, part):
    key = jax.random.fold_in(key, 11)
    return draw_side(key)


def draw_out_grads(key, part):
    key = jax.random.fold_in(key, 23)
    return draw_side(key)


def draw_inverse_slots(key, part):
    shared = 0.0
    diagonals = jnp.stack([side_diagonal(jax.random.fold_in(key, 11), shared), side_diagonal(jax.random.fold_in(key, 23), shared)], axis=1)
    key = jax.random.fold_in(key, 37)
    noise = 0.05 * jax.random.normal(key, (LAYERS, 2, N_GRP, BLK, BLK), jnp.float32)
    symmetric = (noise + jnp.swapaxes(noise, -1, -2)) * BLK ** (-0.5)
    root = diagonals ** (-0.5)
    outer = root[:, :, None, :, None] * root[:, :, None, None, :]
    eye_block = jnp.eye(BLK, dtype=jnp.float32)
    slots = outer * (eye_block + symmetric)
    return slots.reshape(LAYERS, 2, N_GRP * BLK, BLK)


def draw_counts(key, part):
    return count_values(key)


def touch_ends(drawn, key, low, top_value):
    longest = drawn.shape.index(max(drawn.shape))
    spots = []
    for shift in (0, 1):
        where = [jax.random.randint(jax.random.fold_in(key, axis), (), 0, length) for axis, length in enumerate(drawn.shape)]
        where[longest] = (where[longest] + shift) % drawn.shape[longest]
        spots.append(tuple(where))
    return drawn.at[spots[0]].set(low).at[spots[1]].set(top_value)


def scatter_about(rng, dims, width, most, held_as=jnp.bfloat16):
    drawn = jax.random.normal(rng, dims, jnp.float32) * width
    return jnp.minimum(jnp.maximum(drawn, -most), most).astype(held_as)


def setup_inputs(seed: int = 0) -> dict:
    key_list = jax.random.split(jax.random.key(seed), 7)
    activations = draw_activations(jax.random.fold_in(key_list[6], 71), 0)
    out_grads = draw_out_grads(jax.random.fold_in(key_list[6], 71), 0)
    inverse_slots = draw_inverse_slots(jax.random.fold_in(key_list[6], 71), 0)
    gradient = scatter_about(key_list[3], (LAYERS, BLK, BLK), 1.0, 6.0, jnp.float32)
    owners = touch_ends(jax.random.randint(key_list[4], (LAYERS, 2), 0, N_GRP), jax.random.fold_in(key_list[4], 1), 0, N_GRP - 1).astype(jnp.int32)
    counts = draw_counts(jax.random.fold_in(key_list[6], 71), 0)
    return dict(activations=activations, out_grads=out_grads, inverse_slots=inverse_slots, gradient=gradient, owners=owners, counts=counts)


damping = 0.1


def factor_sum(rows, counts):
    position = jnp.arange(TOKENS)
    local = position % TOK_DEV
    limit = jnp.repeat(counts, TOK_DEV)
    keep = (local < limit)[:, None]
    masked = jnp.where(keep, rows, jnp.zeros_like(rows))
    return lax.dot_general(masked, rows, (((0,), (0,)), ((), ())), preferred_element_type=jnp.float32)


def reference(activations, out_grads, inverse_slots, gradient, owners, counts):
    all_tokens = jnp.sum(counts).astype(jnp.float32)
    identity = jnp.eye(BLK, dtype=jnp.float32)
    slot_ids = jnp.arange(N_GRP)
    highest = lax.Precision.HIGHEST
    slot_list = []
    result_list = []
    for layer in range(LAYERS):
        refreshed = []
        for side in range(2):
            source = activations if side == 0 else out_grads
            factor = factor_sum(source[layer], counts) / all_tokens + damping * identity
            owner = owners[layer, side]
            placed = jnp.where((slot_ids == owner)[:, None, None], factor[None], jnp.zeros_like(factor)[None])
            slot_list.append(placed.reshape(N_GRP * BLK, BLK))
            stale = lax.dynamic_slice_in_dim(inverse_slots[layer, side], (owner * BLK).astype(jnp.int32), BLK, 0)
            product = jnp.dot(stale, factor, precision=highest)
            refreshed.append(2.0 * stale - jnp.dot(product, stale, precision=highest))
        left_side = jnp.dot(refreshed[1], gradient[layer], precision=highest)
        result_list.append(jnp.dot(left_side, refreshed[0], precision=highest))
    factor_slots = jnp.stack(slot_list).reshape(LAYERS, 2, N_GRP * BLK, BLK)
    return factor_slots, jnp.stack(result_list)
```

```python
import jax
import jax.numpy as jnp
from jax import lax
from jax.experimental import pallas as pl
from jax.experimental.pallas import tpu as pltpu
from jax.sharding import PartitionSpec as P

MESH = pl.DeviceIdType.MESH
damping = 0.1
BLOCK_AT = (0, 4, 7, 9)


def device(x, y, z, c):
    return (y * 4 + z // 4, (z % 4) * 8 + x * 2 + c)


def high(a, b, dims=(((1,), (0,)), ((), ()))):
    return lax.dot_general(
        a, b, dims, precision=lax.Precision.HIGHEST, preferred_element_type=jnp.float32
    )


def kernel(
    owners, counts, acts, grads, slots, gradient,
    slots_out, pre_out,
    xin, inv, gmat, xsend, xrecv, xcat, terms, near, chunk, near2, part,
    zsend, zrecv, ztenth, zgath, piece, stack, full,
    vmsg, vnear, vown, vcore, vboth, vfar, vpart, vcols, vfull, rows_in, newrows, partner, pblock, pin, fin,
    lsem, xss, xrs, s1, q1, s2, q2, s3, q3, s4, q4, s5, q5,
    sv1, qv1, sv2, qv2, sv3, qv3, sv4, qv4, sf, qf, sr, qr, sp, qp,
):
    grp = lax.axis_index("grp")
    mem = lax.axis_index("mem")
    y = grp // 4
    z = (grp % 4) * 4 + mem // 8
    x = (mem // 2) % 4
    c = mem % 2
    zlo = z % 4
    zhi = z // 4
    layer = z % 2
    zpair = z + 1 - 2 * layer

    def remote(src, dst, ssem, rsem, target):
        return pltpu.make_async_remote_copy(
            src_ref=src, dst_ref=dst, send_sem=ssem, recv_sem=rsem, device_id=target, device_id_type=MESH
        )

    loads = [
        pltpu.make_async_copy(slots, inv, lsem.at[0]),
        pltpu.make_async_copy(acts, xin.at[0], lsem.at[1]),
        pltpu.make_async_copy(grads, xin.at[1], lsem.at[2]),
        pltpu.make_async_copy(gradient.at[layer], gmat, lsem.at[3]),
    ]
    for load in loads:
        load.start()

    core_peer = device(x, y, z, 1 - c)
    plane_peers = [
        (device((x + i) % 4, (y + j) % 4, z, c)) for i in range(4) for j in range(4) if i or j
    ]
    z_peers = [device(x, y, (z + i) % 16, c) for i in range(1, 16)]
    cross_peer = device(x, y, zpair, 1 - c)
    pair_peer = device(x, y, zpair, c)
    barrier = pltpu.get_barrier_semaphore()
    peers = [core_peer, cross_peer] + plane_peers + z_peers
    for peer in peers:
        pl.semaphore_signal(barrier, inc=1, device_id=peer, device_id_type=MESH)

    live = counts[grp * 32 + mem]

    def add(i, totals):
        return tuple(t + counts[i * 8 + k] for k, t in enumerate(totals))

    totals = lax.fori_loop(0, 64, add, (jnp.int32(0),) * 8)
    total = sum(totals[1:], totals[0])
    scale = 1.0 / (jnp.zeros((1, 128), jnp.float32) + total.astype(jnp.float32))

    loads[0].wait()
    for l in range(2):
        for s in range(2):
            mask = jnp.where(owners[l, s] == grp, 1.0, 0.0).astype(jnp.float32)
            for k in range(4):
                vmsg[k, s, l] = inv[l, s, :, 128 * k : 128 * k + 128] * mask
    loads[1].wait()
    loads[2].wait()
    keep = lax.broadcasted_iota(jnp.int32, (128, 512), 0) < live
    for l in range(2):
        xsend[l] = jnp.where(keep, xin[1 - c, l].astype(jnp.float32), 0.0)
        xcat[l, 0:128] = jnp.where(keep, xin[c, l].astype(jnp.float32), 0.0).astype(jnp.bfloat16)
    loads[3].wait()

    pl.semaphore_wait(barrier, len(peers))

    xcopies = [remote(xsend.at[l], xrecv.at[l], xss.at[l], xrs.at[l], core_peer) for l in range(2)]
    for copy in xcopies:
        copy.start()
    v1 = [
        remote(vmsg.at[(y + i) % 4], vnear.at[i - 1], sv1.at[i - 1], qv1.at[i - 1], device(x, (y + i) % 4, z, c))
        for i in range(1, 4)
    ]
    for copy in v1:
        copy.start()

    ring = (
        (x, device((x + 1) % 4, y, z, c), device((x + 3) % 4, y, z, c)),
        (y, device(x, (y + 1) % 4, z, c), device(x, (y + 3) % 4, z, c)),
    )

    def half(l, index, which):
        return pl.ds(pl.multiple_of((index % 4) * 320 + which * 160, 32), 160)

    def send1(l, d, k, index, which):
        copy = remote(
            terms.at[l, half(l, index, which)],
            near.at[l, d, k],
            s1.at[l * 6 + d * 3 + k],
            q1.at[l * 6 + d * 3 + k],
            ring[l][1 + d],
        )
        copy.start()
        return copy

    first = [None, None]
    for l in range(2):
        xcopies[l].wait()
        xcat[l, 128:256] = xrecv[l].astype(jnp.bfloat16)
        for i in range(4):
            block = lax.dot_general(
                xcat[l, :, 128 * i : 128 * i + 128],
                xcat[l, :, 128 * i : 512],
                (((0,), (0,)), ((), ())),
                preferred_element_type=jnp.float32,
            )
            for j in range(4 - i):
                at = (BLOCK_AT[i] + j) * 128
                terms[l, at : at + 128] = block[:, 128 * j : 128 * j + 128]
        p = ring[l][0]
        first[l] = [
            send1(l, 0, 0, p + 2, 0),
            send1(l, 1, 0, p + 2, 1),
            send1(l, 0, 1, p + 1, 1),
            send1(l, 1, 1, p + 3, 0),
        ]

    for copy in v1:
        copy.wait()
    for s in range(2):
        vown[s] = vmsg[y, s] + vnear[0, s] + vnear[1, s] + vnear[2, s]
    v2 = remote(vown.at[1 - c], vcore, sv2.at[0], qv2.at[0], core_peer)
    v2.start()

    for l in range(2):
        p = ring[l][0]
        for d in range(2):
            first[l][d].wait()
            to = half(l, p + (1 if d == 0 else 3), d)
            terms[l, to] = terms[l, to] + near[l, d, 0]
            first[l].append(send1(l, d, 2, p + (1 if d == 0 else 3), d))

    v2.wait()
    for l in range(2):
        vboth[l, c] = vown[c, l]
        vboth[l, 1 - c] = vcore[l]
    v3 = [
        remote(vboth.at[(z + i) % 2], vfar.at[i - 1], sv3.at[i - 1], qv3.at[i - 1], z_peers[i - 1])
        for i in range(1, 16)
    ]
    for copy in v3:
        copy.start()

    second = [[], []]
    for l in range(2):
        for copy in first[l][2:]:
            copy.wait()
        p = ring[l][0]
        chunk[l, 0:160] = terms[l, half(l, p, 0)] + near[l, 0, 2] + near[l, 1, 1]
        chunk[l, 160:320] = terms[l, half(l, p, 1)] + near[l, 0, 1] + near[l, 1, 2]
        q = ring[1 - l][0]
        for i in range(1, 4):
            to = (q + i) % 4
            target = device(x, to, z, c) if l == 0 else device(to, y, z, c)
            copy = remote(
                chunk.at[l, pl.ds(pl.multiple_of(to * 80, 16), 80)],
                near2.at[l, i - 1],
                s2.at[l * 3 + i - 1],
                q2.at[l * 3 + i - 1],
                target,
            )
            copy.start()
            second[l].append(copy)
    for l in range(2):
        for copy in second[l]:
            copy.wait()
        q = ring[1 - l][0]
        part[l] = (
            chunk[l, pl.ds(pl.multiple_of(q * 80, 16), 80)] + near2[l, 0] + near2[l, 1] + near2[l, 2]
        )
    for k in range(16):
        zsend[k] = part[k % 2, 10 * (k // 2) : 10 * (k // 2) + 10]
    third = [
        remote(zsend.at[(z + i) % 16], zrecv.at[i - 1], s3.at[i - 1], q3.at[i - 1], z_peers[i - 1])
        for i in range(1, 16)
    ]
    for i in (8, 7, 9, 6, 10, 5, 11, 4, 12, 3, 13, 2, 14, 1, 15):
        third[i - 1].start()

    for copy in v3:
        copy.wait()
    for r in range(4):
        got = vboth[layer] if r == 0 else vfar[r - 1]
        for i in range(r + 4, 16, 4):
            got = got + vfar[i - 1]
        vpart[(zlo + 4 - r) % 4] = got
    vcols[y, :, x] = vpart[...]
    v4 = [
        remote(vpart, vcols.at[y, :, x], sv4.at[k], qv4.at[k], plane_peers[k]) for k in range(15)
    ]
    for copy in v4:
        copy.start()

    for copy in third:
        copy.wait()
    tenth = zsend[z]
    for i in range(15):
        tenth = tenth + zrecv[i]
    ztenth[...] = tenth * scale
    zgath[z // 2] = ztenth[...]
    fourth = [
        remote(ztenth, zgath.at[z // 2], s4.at[i // 2 - 1], q4.at[i // 2 - 1], z_peers[i - 1])
        for i in range(2, 16, 2)
    ]
    for k in (3, 2, 4, 1, 5, 0, 6):
        fourth[k].start()
    for copy in fourth:
        copy.wait()
    for j in range(8):
        piece[10 * j : 10 * j + 10] = zgath[j]
    mine = jnp.where(layer == 0, x * 4 + y, y * 4 + x)
    at = pl.ds(pl.multiple_of(mine * 80, 16), 80)
    stack[at] = piece[...]
    fifth = [remote(piece, stack.at[at], s5.at[k], q5.at[k], plane_peers[k]) for k in range(15)]
    for copy in fifth:
        copy.start()

    for copy in v4:
        copy.wait()
    for k in range(4):
        vfull[:, 128 * k : 128 * k + 128] = vcols[k].reshape(512, 128)
    row_a = jnp.where(c == 1, (zlo // 2 * 2) * 4 + x, y * 4 + zhi)
    row_b = jnp.where(c == 1, (zlo // 2 * 2 + 1) * 4 + x, y * 4 + zhi)
    rows_in[0:32] = vfull[pl.ds(pl.multiple_of(row_a * 32, 32), 32)]
    rows_in[32:64] = vfull[pl.ds(pl.multiple_of(row_b * 32, 32), 32)]

    for copy in fifth:
        copy.wait()
    diagonal = jnp.where(
        lax.broadcasted_iota(jnp.int32, (128, 128), 0) == lax.broadcasted_iota(jnp.int32, (128, 128), 1),
        damping,
        0.0,
    ).astype(jnp.float32)
    for i in range(4):
        for j in range(i, 4):
            b = (BLOCK_AT[i] + j - i) * 128
            block = stack[b : b + 128]
            if i == j:
                full[128 * i : 128 * i + 128, 128 * j : 128 * j + 128] = block + diagonal
            else:
                full[128 * i : 128 * i + 128, 128 * j : 128 * j + 128] = block
                full[128 * j : 128 * j + 128, 128 * i : 128 * i + 128] = block.T

    def rows_of(plane_lo, core):
        return pl.ds(pl.multiple_of(plane_lo * 128 + x * 32 + core * 16, 16), 16)

    pair_lo = zpair % 4
    fcopies = [
        remote(full.at[rows_of(zlo, 1 - c)], fin.at[layer, c], sf.at[0], qf.at[0], core_peer),
        remote(full.at[rows_of(pair_lo, c)], fin.at[layer, c], sf.at[1], qf.at[1], pair_peer),
        remote(full.at[rows_of(pair_lo, 1 - c)], fin.at[layer, c], sf.at[2], qf.at[2], cross_peer),
    ]
    for copy in fcopies:
        copy.start()
    fin[layer, c] = full[rows_of(zlo, c)]

    half_way = high(rows_in[...], full[...])
    newrows[...] = 2.0 * rows_in[...] - high(half_way, vfull[...])

    rcopy = remote(newrows.at[0:32], partner, sr.at[0], qr.at[0], core_peer)

    @pl.when(c == 0)
    def _():
        rcopy.start()

    targets = [device(x, y, z, 0), device(x, y, zpair, 0), device(x, y, zpair, 1)]
    order = [(layer, 0), (1 - layer, 0), (1 - layer, 1)]
    pcopies = [
        remote(pblock.at[a * 2 + b], pin.at[layer], sp.at[k], qp.at[layer], targets[k])
        for k, (a, b) in enumerate(order)
    ]

    @pl.when(c == 1)
    def _():
        left = high(newrows[...], gmat[...])
        rcopy.wait_recv()
        result = high(left, partner[...], (((1,), (1,)), ((), ())))
        for k in range(4):
            pblock[k] = result[16 * k : 16 * k + 16]
        pin[layer] = pblock[layer * 2 + 1]
        for copy in pcopies:
            copy.start()

    for copy in fcopies:
        copy.wait()
    for l in range(2):
        for s in range(2):
            keep_slot = jnp.where(owners[l, s] == grp, 1.0, 0.0).astype(jnp.float32)
            slots_out[l, s] = fin[l, s] * keep_slot

    @pl.when(c == 0)
    def _():
        rcopy.wait_send()
        remote(pblock.at[0], pin.at[layer], sp.at[0], qp.at[layer], core_peer).wait_recv()

    @pl.when(c == 1)
    def _():
        for copy in pcopies:
            copy.wait_send()

    remote(pblock.at[0], pin.at[1 - layer], sp.at[0], qp.at[1 - layer], core_peer).wait_recv()
    pre_out[...] = pin[...]


def body(activations, out_grads, inverse_slots, gradient, owners, counts):
    f32, bf16 = jnp.float32, jnp.bfloat16
    anywhere = pl.BlockSpec(memory_space=pl.ANY)
    scalars = pl.BlockSpec(memory_space=pltpu.SMEM)
    whole = pl.BlockSpec(memory_space=pltpu.VMEM)
    vm = lambda *shape: pltpu.VMEM(shape, f32)
    dma = lambda n: pltpu.SemaphoreType.DMA((n,))
    return pl.pallas_call(
        kernel,
        out_shape=(
            jax.ShapeDtypeStruct((2, 2, 16, 512), f32),
            jax.ShapeDtypeStruct((2, 16, 32), f32),
        ),
        in_specs=[scalars, scalars, anywhere, anywhere, anywhere, anywhere],
        out_specs=(whole, whole),
        scratch_shapes=[
            pltpu.VMEM((2, 2, 128, 512), bf16),
            vm(2, 2, 16, 512),
            vm(512, 512),
            vm(2, 128, 512),
            vm(2, 128, 512),
            pltpu.VMEM((2, 256, 512), bf16),
            vm(2, 1280, 128),
            vm(2, 2, 3, 160, 128),
            vm(2, 320, 128),
            vm(2, 3, 80, 128),
            vm(2, 80, 128),
            vm(16, 10, 128),
            vm(15, 10, 128),
            vm(10, 128),
            vm(8, 10, 128),
            vm(80, 128),
            vm(1280, 128),
            vm(512, 512),
            vm(4, 2, 2, 16, 128),
            vm(3, 2, 2, 16, 128),
            vm(2, 2, 16, 128),
            vm(2, 16, 128),
            vm(2, 2, 16, 128),
            vm(15, 2, 16, 128),
            vm(4, 2, 16, 128),
            vm(4, 4, 4, 2, 16, 128),
            vm(512, 512),
            vm(64, 512),
            vm(64, 512),
            vm(32, 512),
            vm(4, 16, 32),
            vm(2, 16, 32),
            vm(2, 2, 16, 512),
            dma(4), dma(2), dma(2), dma(12), dma(12), dma(6), dma(6), dma(15), dma(15), dma(7), dma(7),
            dma(15), dma(15),
            dma(3), dma(3), dma(1), dma(1), dma(15), dma(15), dma(15), dma(15), dma(3), dma(3),
            dma(1), dma(1), dma(3), dma(2),
        ],
        compiler_params=pltpu.CompilerParams(
            collective_id=0, has_side_effects=True, vmem_limit_bytes=40 * 1024 * 1024
        ),
    )(owners, counts, activations, out_grads, inverse_slots, gradient)


def solution(mesh):
    placed = (
        P(None, ("grp", "mem"), None),
        P(None, ("grp", "mem"), None),
        P(None, None, ("grp", "mem"), None),
        P(),
        P(),
        P(),
    )
    return jax.shard_map(
        body,
        mesh=mesh,
        in_specs=placed,
        out_specs=(P(None, None, ("grp", "mem"), None), P(None, "mem", "grp")),
        check_vma=False,
    )
```

```python
import jax
import jax.numpy as jnp
from jax import lax
from jax.experimental import pallas as pl
from jax.experimental.pallas import tpu as pltpu
from jax.sharding import PartitionSpec as P

MESH = pl.DeviceIdType.MESH
damping = 0.1


def device(x, y, z, c):
    return (y * 4 + z // 4, (z % 4) * 8 + x * 2 + c)


def split(a):
    top = a.astype(jnp.bfloat16)
    return top, (a - top.astype(jnp.float32)).astype(jnp.bfloat16)


def three(a, b, dims=(((1,), (0,)), ((), ()))):
    one = lambda p, q: lax.dot_general(p, q, dims, preferred_element_type=jnp.float32)
    return one(a[0], b[0]) + (one(a[0], b[1]) + one(a[1], b[0]))


def high(a, b, dims=(((1,), (0,)), ((), ()))):
    return lax.dot_general(
        a, b, dims, precision=lax.Precision.HIGHEST, preferred_element_type=jnp.float32
    )


NEAR_FIRST = (2, 14, 4, 12, 6, 10, 8)
PAIRS = ((0, 1), (0, 2), (0, 3), (1, 2), (1, 3), (2, 3))


def in_half(a, b):
    return (b - a) % 4 < 2 or ((b - a) % 4 == 2 and a < 2)


def kernel(
    owners_in, counts_in, acts, grads, slots, gradient,
    slots_out, pre_out,
    owners, counts, xin, inv, gmat, xsend, xrecv, xcat, terms, near, chunk, near2, part,
    zrecv, unit, zgath, stack, ordered, full,
    vmsg, vnear, vown, vcore, vboth, vfar, vpart, vcols, vfull, rows_in, other_hi, other_lo, base,
    diag_own, diag_far, diag_sum, diag_x,
    newrows, partner, pblock, pin, fin,
    lsem, xss, xrs, s1, q1, s2, q2, s3, q3, s4, q4, s5, q5,
    sv1, qv1, sv2, qv2, sv3, qv3, sv4, qv4, se3, qe3, se4, qe4, sf, qf, sr, qr, sp, qp, ready,
):
    grp = lax.axis_index("grp")
    mem = lax.axis_index("mem")
    y = grp // 4
    z = (grp % 4) * 4 + mem // 8
    x = (mem // 2) % 4
    c = mem % 2
    zlo = z % 4
    zhi = z // 4
    layer = z % 2
    zpair = z + 1 - 2 * layer

    def remote(src, dst, ssem, rsem, target):
        return pltpu.make_async_remote_copy(
            src_ref=src, dst_ref=dst, send_sem=ssem, recv_sem=rsem, device_id=target, device_id_type=MESH
        )

    def signal(sem, peer):
        pl.semaphore_signal(sem, inc=1, device_id=peer, device_id_type=MESH)

    core_peer = device(x, y, z, 1 - c)
    x_peers = [device((x + i) % 4, y, z, c) for i in range(1, 4)]
    y_peers = [device(x, (y + i) % 4, z, c) for i in range(1, 4)]
    plane_shift = [(i, j) for i in range(4) for j in range(4) if i or j]
    plane_peers = [device((x + i) % 4, (y + j) % 4, z, c) for i, j in plane_shift]
    z_peers = [device(x, y, (z + i) % 16, c) for i in range(1, 16)]
    pair_peer = device(x, y, zpair, c)
    cross_peer = device(x, y, zpair, 1 - c)
    barrier = pltpu.get_barrier_semaphore()
    close = [core_peer] + x_peers + y_peers + [z_peers[i - 1] for i in (1, 2, 14, 15)]
    for peer in close:
        signal(barrier, peer)

    loads = [
        pltpu.make_async_copy(counts_in, counts, lsem.at[0]),
        pltpu.make_async_copy(acts, xin.at[0], lsem.at[1]),
        pltpu.make_async_copy(grads, xin.at[1], lsem.at[2]),
        pltpu.make_async_copy(owners_in, owners, lsem.at[3]),
        pltpu.make_async_copy(slots, inv, lsem.at[4]),
        pltpu.make_async_copy(gradient.at[layer], gmat, lsem.at[5]),
    ]
    for load in loads:
        load.start()

    for k in range(3):
        loads[k].wait()
    live = counts[grp * 32 + mem]
    keep = lax.broadcasted_iota(jnp.int32, (128, 512), 0) < live
    for l in range(2):
        theirs = jnp.where(keep, xin[1 - c, l].astype(jnp.float32), 0.0)
        xsend[l] = theirs
        ours = jnp.where(keep, xin[c, l].astype(jnp.float32), 0.0)
        xcat[l, 0:128] = ours.astype(jnp.bfloat16)
        for s, values in ((1 - c, theirs), (c, ours)):
            squares = jnp.sum(values * values, axis=0, keepdims=True)
            for k in range(4):
                vmsg[k, s, l, 16:17] = squares[:, 128:256]
                vmsg[k, s, l, 17:18] = squares[:, 384:512]
    loads[3].wait()
    loads[4].wait()
    for l in range(2):
        for s in range(2):
            mask = jnp.where(owners[l, s] == grp, 1.0, 0.0).astype(jnp.float32)
            for k in range(4):
                vmsg[k, s, l, 0:16] = inv[l, s, :, 128 * k : 128 * k + 128] * mask

    pl.semaphore_wait(barrier, len(close))

    xcopies = [remote(xsend.at[l], xrecv.at[l], xss.at[l], xrs.at[l], core_peer) for l in range(2)]
    for copy in xcopies:
        copy.start()
    signal(ready.at[0], z_peers[1])
    signal(ready.at[0], z_peers[13])
    v1 = [
        remote(vmsg.at[(y + i) % 4], vnear.at[i - 1], sv1.at[i - 1], qv1.at[i - 1], y_peers[i - 1])
        for i in range(1, 4)
    ]
    for copy in v1:
        copy.start()

    where = (x, y)
    across = (x_peers, y_peers)
    at_or_above = lax.broadcasted_iota(jnp.int32, (128, 128), 0) <= lax.broadcasted_iota(
        jnp.int32, (128, 128), 1
    )
    first = [[], []]
    for l in range(2):
        xcopies[l].wait()
        xcat[l, 128:256] = xrecv[l].astype(jnp.bfloat16)
        corner = []
        for i in range(4):
            block = lax.dot_general(
                xcat[l, :, 128 * i : 128 * i + 128],
                xcat[l, :, 128 * i : 512],
                (((0,), (0,)), ((), ())),
                preferred_element_type=jnp.float32,
            )
            corner.append(block[:, 0:128])
            for j in range(i + 1, 4):
                at = 256 + PAIRS.index((i, j)) * 128
                terms[l, at : at + 128] = block[:, 128 * (j - i) : 128 * (j - i) + 128]
        terms[l, 0:128] = jnp.where(at_or_above, corner[0], corner[1])
        terms[l, 128:256] = jnp.where(at_or_above, corner[2], corner[3])
        for i in range(1, 4):
            to = (where[l] + i) % 4
            copy = remote(
                terms.at[l, pl.ds(pl.multiple_of(to * 256, 256), 256)],
                near.at[l, i - 1],
                s1.at[l * 3 + i - 1],
                q1.at[l * 3 + i - 1],
                across[l][i - 1],
            )
            copy.start()
            first[l].append(copy)

    pl.semaphore_wait(ready.at[0], 2)
    signal(ready.at[1], z_peers[3])
    signal(ready.at[1], z_peers[11])

    for copy in v1:
        copy.wait()
    for s in range(2):
        vown[s] = vmsg[y, s] + vnear[0, s] + vnear[1, s] + vnear[2, s]
    v2 = remote(vown.at[1 - c], vcore, sv2.at[0], qv2.at[0], core_peer)
    v2.start()

    def add(i, totals):
        return tuple(t + counts[i * 8 + k] for k, t in enumerate(totals))

    totals = lax.fori_loop(0, 64, add, (jnp.int32(0),) * 8)
    total = sum(totals[1:], totals[0])
    scale = 1.0 / (jnp.zeros((1, 128), jnp.float32) + total.astype(jnp.float32))

    v2.wait()
    for l in range(2):
        vboth[l, c] = vown[c, l, 0:16]
        vboth[l, 1 - c] = vcore[l, 0:16]
        diag_own[l] = vown[c, l, 16:18] + vcore[l, 16:18]
    pl.semaphore_wait(ready.at[1], 2)
    far_first = (8, 7, 9, 6, 10, 5, 11, 4, 12, 3, 13, 2, 14, 1, 15)
    v3 = [
        remote(vboth.at[(z + i) % 2], vfar.at[i - 1], sv3.at[i - 1], qv3.at[i - 1], z_peers[i - 1])
        for i in range(1, 16)
    ]
    e3 = [
        remote(diag_own.at[(z + i) % 2], diag_far.at[i - 1], se3.at[i - 1], qe3.at[i - 1], z_peers[i - 1])
        for i in range(1, 16)
    ]

    def kept(step):
        row = (zlo + 4 - step) % 4
        turn = (y - row + 4) % 4
        return (turn < 2) | ((turn == 2) & (row < 2))

    @pl.when(kept(0))
    def _():
        for i in far_first:
            v3[i - 1].start()

    for i in far_first:
        e3[i - 1].start()

    second = [[], []]
    for l in range(2):
        for copy in first[l]:
            copy.wait()
        own = pl.ds(pl.multiple_of(where[l] * 256, 256), 256)
        chunk[l] = terms[l, own] + near[l, 0] + near[l, 1] + near[l, 2]
        for i in range(1, 4):
            to = (where[1 - l] + i) % 4
            copy = remote(
                chunk.at[l, pl.ds(pl.multiple_of(to * 64, 64), 64)],
                near2.at[l, i - 1],
                s2.at[l * 3 + i - 1],
                q2.at[l * 3 + i - 1],
                across[1 - l][i - 1],
            )
            copy.start()
            second[l].append(copy)
    for l in range(2):
        for copy in second[l]:
            copy.wait()
        own = pl.ds(pl.multiple_of(where[1 - l] * 64, 64), 64)
        part[l] = (chunk[l, own] + near2[l, 0] + near2[l, 1] + near2[l, 2]).reshape(8, 8, 128)
    third = [
        remote(
            part.at[(z + i) % 2, (z + i) % 16 // 2], zrecv.at[i - 1], s3.at[i - 1], q3.at[i - 1], z_peers[i - 1]
        )
        for i in range(1, 16)
    ]
    for i in far_first:
        third[i - 1].start()

    @pl.when(kept(0))
    def _():
        for copy in v3:
            copy.wait_send()

    for r in range(4):

        @pl.when(kept(r))
        def _():
            got = vboth[layer] if r == 0 else None
            for i in range(r or 4, 16, 4):
                v3[i - 1].wait_recv()
                got = vfar[i - 1] if got is None else got + vfar[i - 1]
            vpart[(zlo + 4 - r) % 4] = got

    v4 = []
    for d in range(3):
        row = (y + 4 - d) % 4
        v4.append(
            [
                remote(
                    vpart.at[row], vcols.at[y, row, x], sv4.at[d * 15 + k], qv4.at[d * 15 + k], plane_peers[k]
                )
                for k in range(15)
            ]
        )
    for d in range(2):
        row = (y + 4 - d) % 4
        vcols[y, row, x] = vpart[row]
        for copy in v4[d]:
            copy.start()

    @pl.when(y >= 2)
    def _():
        row = (y + 2) % 4
        vcols[y, row, x] = vpart[row]
        for copy in v4[2]:
            copy.start()

    got = diag_own[layer]
    for i in range(15):
        e3[i].wait()
        got = got + diag_far[i]
    diag_sum[...] = got
    e4 = [remote(diag_sum, diag_x.at[i], se4.at[i], qe4.at[i], x_peers[i]) for i in range(3)]
    for copy in e4:
        copy.start()

    for copy in third:
        copy.wait()
    got = part[layer, z // 2]
    for i in range(15):
        got = got + zrecv[i]
    unit[...] = got * scale
    zgath[0] = unit[...]
    fourth = {
        i: remote(unit, zgath.at[k + 1], s4.at[k], q4.at[k], z_peers[i - 1])
        for k, i in enumerate(NEAR_FIRST)
    }
    for i in (8, 6, 10, 4, 12, 2, 14):
        fourth[i].start()
    mine = jnp.where(layer == 0, x * 4 + y, y * 4 + x)
    fifth = []
    for lo, hi in ((0, 3), (3, 7), (7, 8)):
        for i in NEAR_FIRST[max(lo, 1) - 1 : hi - 1]:
            fourth[i].wait_recv()
        for k in range(15):
            at = len(fifth)
            fifth.append(
                remote(zgath.at[lo:hi], stack.at[mine, lo:hi], s5.at[at], q5.at[at], plane_peers[k])
            )
            fifth[at].start()
    stack[mine] = zgath[...]

    for k, (i, j) in enumerate(plane_shift):
        v4[0][k].wait()
        v4[1][k].wait()

        @pl.when((y + 4 - j) % 4 >= 2)
        def _():
            v4[2][k].wait_recv()

        @pl.when(y >= 2)
        def _():
            v4[2][k].wait_send()

    for a in range(4):
        for b in range(4):
            block = vcols[b, a].reshape(128, 128) if in_half(a, b) else vcols[a, b].reshape(128, 128).T
            vfull[128 * a : 128 * a + 128, 128 * b : 128 * b + 128] = block
    row_a = jnp.where(c == 1, (zlo // 2 * 2) * 4 + x, y * 4 + zhi)
    row_b = jnp.where(c == 1, (zlo // 2 * 2 + 1) * 4 + x, y * 4 + zhi)
    rows_in[0:32] = vfull[pl.ds(pl.multiple_of(row_a * 32, 32), 32)]
    rows_in[32:64] = vfull[pl.ds(pl.multiple_of(row_b * 32, 32), 32)]
    loads[5].wait()

    @pl.when(c == 0)
    def _():
        top, low = split(vfull[...])
        other_hi[...] = top
        other_lo[...] = low
        base[...] = 2.0 * rows_in[...]

    @pl.when(c == 1)
    def _():
        right = split(gmat[...])
        top, low = split(three(split(vfull[...]), right))
        other_hi[...] = top
        other_lo[...] = low
        base[...] = 2.0 * three(split(rows_in[...]), right)

    for copy in e4:
        copy.wait()
    second_diag = (diag_sum[...] + diag_x[0] + diag_x[1] + diag_x[2]) * scale

    for copy in fifth:
        copy.wait()
    for i in NEAR_FIRST:
        fourth[i].wait_send()
    for k, i in enumerate((0,) + NEAR_FIRST):
        at = (z + 16 - i) % 16 // 2
        for p in range(16):
            ordered[p, at] = stack[p, k]

    on_diag = lax.broadcasted_iota(jnp.int32, (128, 128), 0) == lax.broadcasted_iota(jnp.int32, (128, 128), 1)
    eye = jnp.where(on_diag, damping, 0.0).astype(jnp.float32)
    for k in range(2):
        both = ordered[2 * k : 2 * k + 2].reshape(128, 128)
        turned = both.T
        at = 256 * k
        full[at : at + 128, at : at + 128] = jnp.where(at_or_above, both, turned) + eye
        lower = jnp.where(at_or_above, turned, both)
        full[at + 128 : at + 256, at + 128 : at + 256] = (
            jnp.where(on_diag, second_diag[k : k + 1, :], lower) + eye
        )
    for k, (i, j) in enumerate(PAIRS):
        block = ordered[4 + 2 * k : 6 + 2 * k].reshape(128, 128)
        full[128 * i : 128 * i + 128, 128 * j : 128 * j + 128] = block
        full[128 * j : 128 * j + 128, 128 * i : 128 * i + 128] = block.T

    def rows_of(plane_lo, core):
        return pl.ds(pl.multiple_of(plane_lo * 128 + x * 32 + core * 16, 16), 16)

    pair_lo = zpair % 4
    fcopies = [
        remote(full.at[rows_of(zlo, 1 - c)], fin.at[layer, c], sf.at[0], qf.at[0], core_peer),
        remote(full.at[rows_of(pair_lo, c)], fin.at[layer, c], sf.at[1], qf.at[1], pair_peer),
        remote(full.at[rows_of(pair_lo, 1 - c)], fin.at[layer, c], sf.at[2], qf.at[2], cross_peer),
    ]
    for copy in fcopies:
        copy.start()
    fin[layer, c] = full[rows_of(zlo, c)]

    half_way = three(split(rows_in[...]), split(full[...]))
    newrows[...] = base[...] - three(split(half_way), (other_hi[...], other_lo[...]))

    rcopy = remote(newrows.at[0:32], partner, sr.at[0], qr.at[0], core_peer)

    @pl.when(c == 0)
    def _():
        rcopy.start()

    targets = [device(x, y, z, 0), device(x, y, zpair, 0), device(x, y, zpair, 1)]
    order = [(layer, 0), (1 - layer, 0), (1 - layer, 1)]
    pcopies = [
        remote(pblock.at[a * 2 + b], pin.at[layer], sp.at[k], qp.at[layer], targets[k])
        for k, (a, b) in enumerate(order)
    ]

    @pl.when(c == 1)
    def _():
        rcopy.wait_recv()
        result = high(newrows[...], partner[...], (((1,), (1,)), ((), ())))
        for k in range(4):
            pblock[k] = result[16 * k : 16 * k + 16]
        pin[layer] = pblock[layer * 2 + 1]
        for copy in pcopies:
            copy.start()

    for copy in fcopies:
        copy.wait()
    for l in range(2):
        for s in range(2):
            keep_slot = jnp.where(owners[l, s] == grp, 1.0, 0.0).astype(jnp.float32)
            slots_out[l, s] = fin[l, s] * keep_slot

    @pl.when(c == 0)
    def _():
        rcopy.wait_send()
        remote(pblock.at[0], pin.at[layer], sp.at[0], qp.at[layer], core_peer).wait_recv()

    @pl.when(c == 1)
    def _():
        for copy in pcopies:
            copy.wait_send()

    remote(pblock.at[0], pin.at[1 - layer], sp.at[0], qp.at[1 - layer], core_peer).wait_recv()
    pre_out[...] = pin[...]


def body(activations, out_grads, inverse_slots, gradient, owners, counts):
    f32, bf16 = jnp.float32, jnp.bfloat16
    whole = pl.BlockSpec(memory_space=pltpu.VMEM)
    vm = lambda *shape: pltpu.VMEM(shape, f32)
    dma = lambda n: pltpu.SemaphoreType.DMA((n,))
    return pl.pallas_call(
        kernel,
        out_shape=(
            jax.ShapeDtypeStruct((2, 2, 16, 512), f32),
            jax.ShapeDtypeStruct((2, 16, 32), f32),
        ),
        in_specs=[pl.BlockSpec(memory_space=pltpu.HBM)] * 6,
        out_specs=(whole, whole),
        scratch_shapes=[
            pltpu.SMEM((2, 2), jnp.int32),
            pltpu.SMEM((512,), jnp.int32),
            pltpu.VMEM((2, 2, 128, 512), bf16),
            vm(2, 2, 16, 512),
            vm(512, 512),
            vm(2, 128, 512),
            vm(2, 128, 512),
            pltpu.VMEM((2, 256, 512), bf16),
            vm(2, 1024, 128),
            vm(2, 3, 256, 128),
            vm(2, 256, 128),
            vm(2, 3, 64, 128),
            vm(2, 8, 8, 128),
            vm(15, 8, 128),
            vm(8, 128),
            vm(8, 8, 128),
            vm(16, 8, 8, 128),
            vm(16, 8, 8, 128),
            vm(512, 512),
            vm(4, 2, 2, 18, 128),
            vm(3, 2, 2, 18, 128),
            vm(2, 2, 18, 128),
            vm(2, 18, 128),
            vm(2, 2, 16, 128),
            vm(15, 2, 16, 128),
            vm(4, 2, 16, 128),
            vm(4, 4, 4, 2, 16, 128),
            vm(512, 512),
            vm(64, 512),
            pltpu.VMEM((512, 512), bf16),
            pltpu.VMEM((512, 512), bf16),
            vm(64, 512),
            vm(2, 2, 128),
            vm(15, 2, 128),
            vm(2, 128),
            vm(3, 2, 128),
            vm(64, 512),
            vm(32, 512),
            vm(4, 16, 32),
            vm(2, 16, 32),
            vm(2, 2, 16, 512),
            dma(6), dma(2), dma(2), dma(6), dma(6), dma(6), dma(6), dma(15), dma(15), dma(7), dma(7),
            dma(45), dma(45),
            dma(3), dma(3), dma(1), dma(1), dma(15), dma(15), dma(45), dma(45), dma(15), dma(15), dma(3), dma(3),
            dma(3), dma(3), dma(1), dma(1), dma(3), dma(2),
            pltpu.SemaphoreType.REGULAR((2,)),
        ],
        compiler_params=pltpu.CompilerParams(
            collective_id=0, has_side_effects=True, vmem_limit_bytes=62 * 1024 * 1024
        ),
    )(owners, counts, activations, out_grads, inverse_slots, gradient)


def solution(mesh):
    placed = (
        P(None, ("grp", "mem"), None),
        P(None, ("grp", "mem"), None),
        P(None, None, ("grp", "mem"), None),
        P(),
        P(),
        P(),
    )
    return jax.shard_map(
        body,
        mesh=mesh,
        in_specs=placed,
        out_specs=(P(None, None, ("grp", "mem"), None), P(None, "mem", "grp")),
        check_vma=False,
    )
```

```python
import jax
import jax.numpy as jnp
from jax import lax
from jax.experimental import pallas as pl
from jax.experimental.pallas import tpu as pltpu
from jax.sharding import PartitionSpec as P

MESH = pl.DeviceIdType.MESH
damping = 0.1


def device(x, y, z, c):
    return (y * 4 + z // 4, (z % 4) * 8 + x * 2 + c)


def split(a):
    top = a.astype(jnp.bfloat16)
    return top, (a - top.astype(jnp.float32)).astype(jnp.bfloat16)


def three(a, b, dims=(((1,), (0,)), ((), ()))):
    one = lambda p, q: lax.dot_general(p, q, dims, preferred_element_type=jnp.float32)
    return one(a[0], b[0]) + (one(a[0], b[1]) + one(a[1], b[0]))


NEAR_FIRST = (2, 14, 4, 12, 6, 10, 8)
PAIRS = ((0, 1), (0, 2), (0, 3), (1, 2), (1, 3), (2, 3))


def in_half(a, b):
    return (b - a) % 4 < 2 or ((b - a) % 4 == 2 and a < 2)


def kernel(
    owners_in, counts_in, acts, grads, slots, gradient,
    slots_out, pre_out,
    owners, counts, xin, inv, gmat, xsend, xrecv, xcat, terms, near, chunk, near2, part,
    zrecv, unit, zgath, stack, ordered, full,
    vmsg, vnear, vown, vcore, vboth, vfar, vpart, vcols, vfull, rows_in, other_hi, other_lo, base,
    diag_own, diag_far, diag_sum, diag_x,
    newrows, partner, pblock, pin, fin,
    lsem, xss, xrs, s1, q1, s2, q2, s3, q3, s4, q4, s5, q5,
    sv1, qv1, sv2, qv2, sv3, qv3, sv4, qv4, se3, qe3, se4, qe4, sf, qf, sr, qr, sp, qp, ready,
):
    grp = lax.axis_index("grp")
    mem = lax.axis_index("mem")
    y = grp // 4
    z = (grp % 4) * 4 + mem // 8
    x = (mem // 2) % 4
    c = mem % 2
    zlo = z % 4
    zhi = z // 4
    layer = z % 2
    zpair = z + 1 - 2 * layer

    def remote(src, dst, ssem, rsem, target):
        return pltpu.make_async_remote_copy(
            src_ref=src, dst_ref=dst, send_sem=ssem, recv_sem=rsem, device_id=target, device_id_type=MESH
        )

    def signal(sem, peer):
        pl.semaphore_signal(sem, inc=1, device_id=peer, device_id_type=MESH)

    core_peer = device(x, y, z, 1 - c)
    x_peers = [device((x + i) % 4, y, z, c) for i in range(1, 4)]
    y_peers = [device(x, (y + i) % 4, z, c) for i in range(1, 4)]
    plane_shift = sorted(
        [(i, j) for i in range(4) for j in range(4) if i or j], key=lambda at: -(min(at[0], 4 - at[0]) + min(at[1], 4 - at[1]))
    )
    plane_peers = [device((x + i) % 4, (y + j) % 4, z, c) for i, j in plane_shift]
    z_peers = [device(x, y, (z + i) % 16, c) for i in range(1, 16)]
    pair_peer = device(x, y, zpair, c)
    cross_peer = device(x, y, zpair, 1 - c)
    barrier = pltpu.get_barrier_semaphore()
    beside = [x_peers[0], x_peers[2], y_peers[0], y_peers[2], z_peers[0], z_peers[14]]
    close = [core_peer] + beside
    for peer in close:
        signal(barrier, peer)

    loads = [
        pltpu.make_async_copy(counts_in, counts, lsem.at[0]),
        pltpu.make_async_copy(acts, xin.at[0], lsem.at[1]),
        pltpu.make_async_copy(grads, xin.at[1], lsem.at[2]),
        pltpu.make_async_copy(owners_in, owners, lsem.at[3]),
        pltpu.make_async_copy(slots, inv, lsem.at[4]),
        pltpu.make_async_copy(gradient.at[layer], gmat, lsem.at[5]),
    ]
    for load in loads:
        load.start()

    for k in range(3):
        loads[k].wait()
    live = counts[grp * 32 + mem]
    keep = lax.broadcasted_iota(jnp.int32, (128, 512), 0) < live
    for l in range(2):
        theirs = jnp.where(keep, xin[1 - c, l].astype(jnp.float32), 0.0)
        xsend[l] = theirs.T
        ours = jnp.where(keep, xin[c, l].astype(jnp.float32), 0.0)
        xcat[l, :, 0:128] = ours.T.astype(jnp.bfloat16)
        for s, values in ((1 - c, theirs), (c, ours)):
            squares = jnp.sum(values * values, axis=0, keepdims=True)
            for k in range(4):
                vmsg[k, s, l, 16:17] = squares[:, 128:256]
                vmsg[k, s, l, 17:18] = squares[:, 384:512]
    loads[3].wait()
    loads[4].wait()
    for l in range(2):
        for s in range(2):
            mask = jnp.where(owners[l, s] == grp, 1.0, 0.0).astype(jnp.float32)
            for k in range(4):
                vmsg[k, s, l, 0:16] = inv[l, s, :, 128 * k : 128 * k + 128] * mask

    pl.semaphore_wait(barrier, len(close))

    xcopies = [remote(xsend.at[l], xrecv.at[l], xss.at[l], xrs.at[l], core_peer) for l in range(2)]
    for copy in xcopies:
        copy.start()
    for peer in beside:
        signal(ready.at[0], peer)
    v1 = [
        remote(vmsg.at[(y + i) % 4], vnear.at[i - 1], sv1.at[i - 1], qv1.at[i - 1], y_peers[i - 1])
        for i in range(1, 4)
    ]

    where = (x, y)
    across = (x_peers, y_peers)
    at_or_above = lax.broadcasted_iota(jnp.int32, (128, 128), 0) <= lax.broadcasted_iota(
        jnp.int32, (128, 128), 1
    )
    first = [[], []]
    for l in range(2):
        xcopies[l].wait()
        xcat[l, :, 128:256] = xrecv[l].astype(jnp.bfloat16)
        right = [
            lax.dot_general(
                xcat[l, 0 : 256 + 256 * k],
                xcat[l, 256 * k : 256 * k + 256],
                (((1,), (1,)), ((), ())),
                preferred_element_type=jnp.float32,
            )
            for k in range(2)
        ]

        def pair(i, j):
            return right[j // 2][128 * i : 128 * i + 128, 128 * (j % 2) : 128 * (j % 2) + 128]

        terms[l, 0:128] = jnp.where(at_or_above, pair(0, 0), pair(1, 1))
        terms[l, 128:256] = jnp.where(at_or_above, pair(2, 2), pair(3, 3))
        for k, (i, j) in enumerate(PAIRS):
            terms[l, 256 + 128 * k : 384 + 128 * k] = pair(i, j)
        if l == 0:
            pl.semaphore_wait(ready.at[0], len(beside))
        for i in (2, 1, 3):
            to = (where[l] + i) % 4
            copy = remote(
                terms.at[l, pl.ds(pl.multiple_of(to * 256, 256), 256)],
                near.at[l, i - 1],
                s1.at[l * 3 + i - 1],
                q1.at[l * 3 + i - 1],
                across[l][i - 1],
            )
            copy.start()
            first[l].append(copy)
        if l == 0:
            signal(ready.at[1], z_peers[1])
            signal(ready.at[1], z_peers[13])
            for i in (2, 1, 3):
                v1[i - 1].start()

    pl.semaphore_wait(ready.at[1], 2)
    signal(ready.at[2], z_peers[3])
    signal(ready.at[2], z_peers[11])

    for copy in v1:
        copy.wait()
    for s in range(2):
        vown[s] = vmsg[y, s] + vnear[0, s] + vnear[1, s] + vnear[2, s]
    v2 = remote(vown.at[1 - c], vcore, sv2.at[0], qv2.at[0], core_peer)
    v2.start()

    def add(i, totals):
        return tuple(t + counts[i * 8 + k] for k, t in enumerate(totals))

    totals = lax.fori_loop(0, 64, add, (jnp.int32(0),) * 8)
    total = sum(totals[1:], totals[0])
    scale = 1.0 / (jnp.zeros((1, 128), jnp.float32) + total.astype(jnp.float32))

    v2.wait()
    for l in range(2):
        vboth[l, c] = vown[c, l, 0:16]
        vboth[l, 1 - c] = vcore[l, 0:16]
        diag_own[l] = vown[c, l, 16:18] + vcore[l, 16:18]
    pl.semaphore_wait(ready.at[2], 2)
    far_first = (8, 7, 9, 6, 10, 5, 11, 4, 12, 3, 13, 2, 14, 1, 15)
    v3 = [
        remote(vboth.at[(z + i) % 2], vfar.at[i - 1], sv3.at[i - 1], qv3.at[i - 1], z_peers[i - 1])
        for i in range(1, 16)
    ]
    e3 = [
        remote(diag_own.at[(z + i) % 2], diag_far.at[i - 1], se3.at[i - 1], qe3.at[i - 1], z_peers[i - 1])
        for i in range(1, 16)
    ]

    def kept(step):
        row = (zlo + 4 - step) % 4
        turn = (y - row + 4) % 4
        return (turn < 2) | ((turn == 2) & (row < 2))

    @pl.when(kept(0))
    def _():
        for i in far_first:
            v3[i - 1].start()

    for i in far_first:
        e3[i - 1].start()

    second = [[], []]
    for l in range(2):
        for copy in first[l]:
            copy.wait()
        own = pl.ds(pl.multiple_of(where[l] * 256, 256), 256)
        chunk[l] = terms[l, own] + near[l, 0] + near[l, 1] + near[l, 2]
        for i in (2, 1, 3):
            to = (where[1 - l] + i) % 4
            copy = remote(
                chunk.at[l, pl.ds(pl.multiple_of(to * 64, 64), 64)],
                near2.at[l, i - 1],
                s2.at[l * 3 + i - 1],
                q2.at[l * 3 + i - 1],
                across[1 - l][i - 1],
            )
            copy.start()
            second[l].append(copy)
    for l in range(2):
        for copy in second[l]:
            copy.wait()
        own = pl.ds(pl.multiple_of(where[1 - l] * 64, 64), 64)
        part[l] = (chunk[l, own] + near2[l, 0] + near2[l, 1] + near2[l, 2]).reshape(8, 8, 128)
    third = [
        remote(
            part.at[(z + i) % 2, (z + i) % 16 // 2], zrecv.at[i - 1], s3.at[i - 1], q3.at[i - 1], z_peers[i - 1]
        )
        for i in range(1, 16)
    ]
    for i in far_first:
        third[i - 1].start()

    @pl.when(kept(0))
    def _():
        for copy in v3:
            copy.wait_send()

    for r in range(4):

        @pl.when(kept(r))
        def _():
            got = vboth[layer] if r == 0 else None
            for i in range(r or 4, 16, 4):
                v3[i - 1].wait_recv()
                got = vfar[i - 1] if got is None else got + vfar[i - 1]
            vpart[(zlo + 4 - r) % 4] = got

    v4 = []
    for d in range(3):
        row = (y + 4 - d) % 4
        v4.append(
            [
                remote(
                    vpart.at[row], vcols.at[y, row, x], sv4.at[d * 15 + k], qv4.at[d * 15 + k], plane_peers[k]
                )
                for k in range(15)
            ]
        )
    for d in range(2):
        row = (y + 4 - d) % 4
        vcols[y, row, x] = vpart[row]
        for copy in v4[d]:
            copy.start()

    @pl.when(y >= 2)
    def _():
        row = (y + 2) % 4
        vcols[y, row, x] = vpart[row]
        for copy in v4[2]:
            copy.start()

    got = diag_own[layer]
    for i in range(15):
        e3[i].wait()
        got = got + diag_far[i]
    diag_sum[...] = got
    e4 = [remote(diag_sum, diag_x.at[i], se4.at[i], qe4.at[i], x_peers[i]) for i in range(3)]
    for copy in e4:
        copy.start()

    for copy in third:
        copy.wait()
    got = part[layer, z // 2]
    for i in range(15):
        got = got + zrecv[i]
    unit[...] = got * scale
    zgath[0] = unit[...]
    fourth = {
        i: remote(unit, zgath.at[k + 1], s4.at[k], q4.at[k], z_peers[i - 1])
        for k, i in enumerate(NEAR_FIRST)
    }
    for i in (8, 6, 10, 4, 12, 2, 14):
        fourth[i].start()
    mine = jnp.where(layer == 0, x * 4 + y, y * 4 + x)
    fifth = []
    straight = []
    for k in range(5):
        i, j = plane_shift[k]
        straight.append(
            remote(
                unit, stack.at[mine, 7], s5.at[45 + k], q5.at[45 + k], device((x + i) % 4, (y + j) % 4, (z + 8) % 16, c)
            )
        )
        straight[k].start()
    for lo, hi in ((0, 3), (3, 7), (7, 8)):
        for i in NEAR_FIRST[max(lo, 1) - 1 : hi - 1]:
            fourth[i].wait_recv()
        for k in range(5 if lo == 7 else 0, 15):
            at = len(fifth)
            fifth.append(
                remote(zgath.at[lo:hi], stack.at[mine, lo:hi], s5.at[at], q5.at[at], plane_peers[k])
            )
            fifth[at].start()
    stack[mine] = zgath[...]

    for k, (i, j) in enumerate(plane_shift):
        v4[0][k].wait()
        v4[1][k].wait()

        @pl.when((y + 4 - j) % 4 >= 2)
        def _():
            v4[2][k].wait_recv()

        @pl.when(y >= 2)
        def _():
            v4[2][k].wait_send()

    for a in range(4):
        for b in range(4):
            block = vcols[b, a].reshape(128, 128) if in_half(a, b) else vcols[a, b].reshape(128, 128).T
            vfull[128 * a : 128 * a + 128, 128 * b : 128 * b + 128] = block
    row_a = jnp.where(c == 1, (zlo // 2 * 2) * 4 + x, y * 4 + zhi)
    row_b = jnp.where(c == 1, (zlo // 2 * 2 + 1) * 4 + x, y * 4 + zhi)
    rows_in[0:32] = vfull[pl.ds(pl.multiple_of(row_a * 32, 32), 32)]
    rows_in[32:64] = vfull[pl.ds(pl.multiple_of(row_b * 32, 32), 32)]
    loads[5].wait()

    @pl.when(c == 0)
    def _():
        top, low = split(vfull[...])
        other_hi[...] = top
        other_lo[...] = low
        base[...] = 2.0 * rows_in[...]

    @pl.when(c == 1)
    def _():
        right = split(gmat[...])
        top, low = split(three(split(vfull[...]), right))
        other_hi[...] = top
        other_lo[...] = low
        base[...] = 2.0 * three(split(rows_in[...]), right)

    for copy in e4:
        copy.wait()
    second_diag = (diag_sum[...] + diag_x[0] + diag_x[1] + diag_x[2]) * scale

    for copy in fifth + straight:
        copy.wait()
    for i in NEAR_FIRST:
        fourth[i].wait_send()
    for k, i in enumerate((0,) + NEAR_FIRST):
        at = (z + 16 - i) % 16 // 2
        for p in range(16):
            ordered[p, at] = stack[p, k]

    on_diag = lax.broadcasted_iota(jnp.int32, (128, 128), 0) == lax.broadcasted_iota(jnp.int32, (128, 128), 1)
    eye = jnp.where(on_diag, damping, 0.0).astype(jnp.float32)
    for k in range(2):
        both = ordered[2 * k : 2 * k + 2].reshape(128, 128)
        turned = both.T
        at = 256 * k
        full[at : at + 128, at : at + 128] = jnp.where(at_or_above, both, turned) + eye
        lower = jnp.where(at_or_above, turned, both)
        full[at + 128 : at + 256, at + 128 : at + 256] = (
            jnp.where(on_diag, second_diag[k : k + 1, :], lower) + eye
        )
    for k, (i, j) in enumerate(PAIRS):
        block = ordered[4 + 2 * k : 6 + 2 * k].reshape(128, 128)
        full[128 * i : 128 * i + 128, 128 * j : 128 * j + 128] = block
        full[128 * j : 128 * j + 128, 128 * i : 128 * i + 128] = block.T

    def rows_of(plane_lo, core):
        return pl.ds(pl.multiple_of(plane_lo * 128 + x * 32 + core * 16, 16), 16)

    pair_lo = zpair % 4
    fcopies = [
        remote(full.at[rows_of(zlo, 1 - c)], fin.at[layer, c], sf.at[0], qf.at[0], core_peer),
        remote(full.at[rows_of(pair_lo, c)], fin.at[layer, c], sf.at[1], qf.at[1], pair_peer),
        remote(full.at[rows_of(pair_lo, 1 - c)], fin.at[layer, c], sf.at[2], qf.at[2], cross_peer),
    ]
    for copy in fcopies:
        copy.start()
    fin[layer, c] = full[rows_of(zlo, c)]

    half_way = three(split(rows_in[...]), split(full[...]))
    newrows[...] = base[...] - three(split(half_way), (other_hi[...], other_lo[...]))

    rcopy = remote(newrows.at[0:32], partner, sr.at[0], qr.at[0], core_peer)

    @pl.when(c == 0)
    def _():
        rcopy.start()

    targets = [device(x, y, z, 0), device(x, y, zpair, 0), device(x, y, zpair, 1)]
    order = [(layer, 0), (1 - layer, 0), (1 - layer, 1)]
    pcopies = [
        remote(pblock.at[a * 2 + b], pin.at[layer], sp.at[k], qp.at[layer], targets[k])
        for k, (a, b) in enumerate(order)
    ]

    @pl.when(c == 1)
    def _():
        rcopy.wait_recv()
        result = three(split(newrows[...]), split(partner[...]), (((1,), (1,)), ((), ())))
        for k in range(4):
            pblock[k] = result[16 * k : 16 * k + 16]
        pin[layer] = pblock[layer * 2 + 1]
        for copy in pcopies:
            copy.start()

    for copy in fcopies:
        copy.wait()
    for l in range(2):
        for s in range(2):
            keep_slot = jnp.where(owners[l, s] == grp, 1.0, 0.0).astype(jnp.float32)
            slots_out[l, s] = fin[l, s] * keep_slot

    @pl.when(c == 0)
    def _():
        rcopy.wait_send()
        remote(pblock.at[0], pin.at[layer], sp.at[0], qp.at[layer], core_peer).wait_recv()

    @pl.when(c == 1)
    def _():
        for copy in pcopies:
            copy.wait_send()

    remote(pblock.at[0], pin.at[1 - layer], sp.at[0], qp.at[1 - layer], core_peer).wait_recv()
    pre_out[...] = pin[...]


def body(activations, out_grads, inverse_slots, gradient, owners, counts):
    f32, bf16 = jnp.float32, jnp.bfloat16
    whole = pl.BlockSpec(memory_space=pltpu.VMEM)
    vm = lambda *shape: pltpu.VMEM(shape, f32)
    dma = lambda n: pltpu.SemaphoreType.DMA((n,))
    operands = (owners, counts, activations, out_grads, inverse_slots, gradient)
    return pl.pallas_call(
        kernel,
        out_shape=(
            jax.ShapeDtypeStruct((2, 2, 16, 512), f32),
            jax.ShapeDtypeStruct((2, 16, 32), f32),
        ),
        in_specs=[pl.BlockSpec(memory_space=pltpu.HBM)] * 6,
        out_specs=(whole, whole),
        scratch_shapes=[
            pltpu.SMEM((2, 2), jnp.int32),
            pltpu.SMEM((512,), jnp.int32),
            pltpu.VMEM((2, 2, 128, 512), bf16),
            vm(2, 2, 16, 512),
            vm(512, 512),
            vm(2, 512, 128),
            vm(2, 512, 128),
            pltpu.VMEM((2, 512, 256), bf16),
            vm(2, 1024, 128),
            vm(2, 3, 256, 128),
            vm(2, 256, 128),
            vm(2, 3, 64, 128),
            vm(2, 8, 8, 128),
            vm(15, 8, 128),
            vm(8, 128),
            vm(8, 8, 128),
            vm(16, 8, 8, 128),
            vm(16, 8, 8, 128),
            vm(512, 512),
            vm(4, 2, 2, 18, 128),
            vm(3, 2, 2, 18, 128),
            vm(2, 2, 18, 128),
            vm(2, 18, 128),
            vm(2, 2, 16, 128),
            vm(15, 2, 16, 128),
            vm(4, 2, 16, 128),
            vm(4, 4, 4, 2, 16, 128),
            vm(512, 512),
            vm(64, 512),
            pltpu.VMEM((512, 512), bf16),
            pltpu.VMEM((512, 512), bf16),
            vm(64, 512),
            vm(2, 2, 128),
            vm(15, 2, 128),
            vm(2, 128),
            vm(3, 2, 128),
            vm(64, 512),
            vm(32, 512),
            vm(4, 16, 32),
            vm(2, 16, 32),
            vm(2, 2, 16, 512),
            dma(6), dma(2), dma(2), dma(6), dma(6), dma(6), dma(6), dma(15), dma(15), dma(7), dma(7),
            dma(50), dma(50),
            dma(3), dma(3), dma(1), dma(1), dma(15), dma(15), dma(45), dma(45), dma(15), dma(15), dma(3), dma(3),
            dma(3), dma(3), dma(1), dma(1), dma(3), dma(2),
            pltpu.SemaphoreType.REGULAR((3,)),
        ],
        compiler_params=pltpu.CompilerParams(
            collective_id=0, has_side_effects=True, vmem_limit_bytes=40 * 1024 * 1024
        ),
    )(*(pltpu.with_memory_space_constraint(a, pltpu.HBM) for a in operands))


def solution(mesh):
    placed = (
        P(None, ("grp", "mem"), None),
        P(None, ("grp", "mem"), None),
        P(None, None, ("grp", "mem"), None),
        P(),
        P(),
        P(),
    )
    return jax.shard_map(
        body,
        mesh=mesh,
        in_specs=placed,
        out_specs=(P(None, None, ("grp", "mem"), None), P(None, "mem", "grp")),
        check_vma=False,
    )
```

```python
import jax
import jax.numpy as jnp
from jax import lax
from jax.experimental import pallas as pl
from jax.experimental.pallas import tpu as pltpu
from jax.sharding import PartitionSpec as P

MESH = pl.DeviceIdType.MESH
damping = 0.1


def device(x, y, z, c):
    return (y * 4 + z // 4, (z % 4) * 8 + x * 2 + c)


def split(a):
    top = a.astype(jnp.bfloat16)
    return top, (a - top.astype(jnp.float32)).astype(jnp.bfloat16)


def three(a, b, dims=(((1,), (0,)), ((), ()))):
    one = lambda p, q: lax.dot_general(p, q, dims, preferred_element_type=jnp.float32)
    return one(a[0], b[0]) + (one(a[0], b[1]) + one(a[1], b[0]))


NEAR_FIRST = (2, 14, 4, 12, 6, 10, 8)
PAIRS = ((0, 1), (0, 2), (0, 3), (1, 2), (1, 3), (2, 3))


def kernel(
    owners_in, counts_in, acts, grads, slots, gradient,
    slots_out, pre_out,
    owners, counts, xin, inv, gmat, xsend, xrecv, xcat, terms, near, chunk, near2, part,
    zrecv, unit, zgath, stack, ordered, full,
    vmsg, vnear, vown, vcore, vboth, vfar, vpart, vcols, vfull, rows_in, other_hi, other_lo, base,
    diag_own, diag_far, diag_sum, diag_x,
    newrows, partner, pblock, pin, fin,
    lsem, xss, xrs, s1, q1, s2, q2, s3, q3, s4, q4, s5, q5,
    sv1, qv1, sv2, qv2, sv3, qv3, sv4, qv4, se3, qe3, se4, qe4, sf, qf, sr, qr, sp, qp, ready,
):
    grp = lax.axis_index("grp")
    mem = lax.axis_index("mem")
    y = grp // 4
    z = (grp % 4) * 4 + mem // 8
    x = (mem // 2) % 4
    c = mem % 2
    zlo = z % 4
    zhi = z // 4
    layer = z % 2
    zpair = z + 1 - 2 * layer

    def remote(src, dst, ssem, rsem, target):
        return pltpu.make_async_remote_copy(
            src_ref=src, dst_ref=dst, send_sem=ssem, recv_sem=rsem, device_id=target, device_id_type=MESH
        )

    def signal(sem, peer):
        pl.semaphore_signal(sem, inc=1, device_id=peer, device_id_type=MESH)

    core_peer = device(x, y, z, 1 - c)
    x_peers = [device((x + i) % 4, y, z, c) for i in range(1, 4)]
    y_peers = [device(x, (y + i) % 4, z, c) for i in range(1, 4)]
    plane_shift = sorted(
        [(i, j) for i in range(4) for j in range(4) if i or j], key=lambda at: -(min(at[0], 4 - at[0]) + min(at[1], 4 - at[1]))
    )
    plane_peers = [device((x + i) % 4, (y + j) % 4, z, c) for i, j in plane_shift]
    z_peers = [device(x, y, (z + i) % 16, c) for i in range(1, 16)]
    pair_peer = device(x, y, zpair, c)
    cross_peer = device(x, y, zpair, 1 - c)
    barrier = pltpu.get_barrier_semaphore()
    close = [core_peer] + x_peers + y_peers + [z_peers[i - 1] for i in (1, 2, 14, 15)]
    for peer in close:
        signal(barrier, peer)

    loads = [
        pltpu.make_async_copy(counts_in, counts, lsem.at[0]),
        pltpu.make_async_copy(acts, xin.at[0], lsem.at[1]),
        pltpu.make_async_copy(grads, xin.at[1], lsem.at[2]),
        pltpu.make_async_copy(owners_in, owners, lsem.at[3]),
        pltpu.make_async_copy(slots, inv, lsem.at[4]),
        pltpu.make_async_copy(gradient.at[layer], gmat, lsem.at[5]),
    ]
    for load in loads:
        load.start()

    for k in range(3):
        loads[k].wait()
    live = counts[grp * 32 + mem]
    keep = lax.broadcasted_iota(jnp.int32, (128, 512), 0) < live
    for l in range(2):
        theirs = jnp.where(keep, xin[1 - c, l].astype(jnp.float32), 0.0)
        xsend[l] = theirs.T
        ours = jnp.where(keep, xin[c, l].astype(jnp.float32), 0.0)
        xcat[l, :, 0:128] = ours.T.astype(jnp.bfloat16)
        for s, values in ((1 - c, theirs), (c, ours)):
            squares = jnp.sum(values * values, axis=0, keepdims=True)
            for k in range(4):
                vmsg[k, s, l, 16:17] = squares[:, 128:256]
                vmsg[k, s, l, 17:18] = squares[:, 384:512]
    loads[3].wait()
    loads[4].wait()
    for l in range(2):
        for s in range(2):
            mask = jnp.where(owners[l, s] == grp, 1.0, 0.0).astype(jnp.float32)
            for k in range(4):
                vmsg[k, s, l, 0:16] = inv[l, s, :, 128 * k : 128 * k + 128] * mask

    pl.semaphore_wait(barrier, len(close))

    xcopies = [remote(xsend.at[l], xrecv.at[l], xss.at[l], xrs.at[l], core_peer) for l in range(2)]
    for copy in xcopies:
        copy.start()
    signal(ready.at[0], z_peers[1])
    signal(ready.at[0], z_peers[13])
    v1 = [
        remote(vmsg.at[(y + i) % 4], vnear.at[i - 1], sv1.at[i - 1], qv1.at[i - 1], y_peers[i - 1])
        for i in range(1, 4)
    ]

    for copy in v1:
        copy.start()
    where = (x, y)
    across = (x_peers, y_peers)
    at_or_above = lax.broadcasted_iota(jnp.int32, (128, 128), 0) <= lax.broadcasted_iota(
        jnp.int32, (128, 128), 1
    )
    turn_to = jnp.where(zlo < 2, 1, 3)
    quads = [(zhi + 2) % 4, (zhi + turn_to) % 4, (zhi + 4 - turn_to) % 4, zhi]
    first = [[[] for _ in range(4)] for _ in range(2)]
    for l in range(2):
        xcopies[l].wait()
        xcat[l, :, 128:256] = xrecv[l].astype(jnp.bfloat16)
        right = [
            lax.dot_general(
                xcat[l, 0 : 256 + 256 * k],
                xcat[l, 256 * k : 256 * k + 256],
                (((1,), (1,)), ((), ())),
                preferred_element_type=jnp.float32,
            )
            for k in range(2)
        ]

        def pair(i, j):
            return right[j // 2][128 * i : 128 * i + 128, 128 * (j % 2) : 128 * (j % 2) + 128]

        terms[l, 0, 0:2] = jnp.where(at_or_above, pair(0, 0), pair(1, 1)).reshape(2, 8, 8, 128)
        terms[l, 0, 2:4] = jnp.where(at_or_above, pair(2, 2), pair(3, 3)).reshape(2, 8, 8, 128)
        for k, (i, j) in enumerate(PAIRS):
            b = k + 2
            terms[l, b // 2, b % 2 * 2 : b % 2 * 2 + 2] = pair(i, j).reshape(2, 8, 8, 128)
        for t in range(4):
            for i in (2, 1, 3):
                at = (l * 4 + t) * 3 + i - 1
                copy = remote(
                    terms.at[l, (where[l] + i) % 4, :, pl.ds(quads[t] * 2, 2)],
                    near.at[l, t, i - 1],
                    s1.at[at],
                    q1.at[at],
                    across[l][i - 1],
                )
                copy.start()
                first[l][t].append(copy)

    pl.semaphore_wait(ready.at[0], 2)
    signal(ready.at[1], z_peers[3])
    signal(ready.at[1], z_peers[11])

    for copy in v1:
        copy.wait()
    for s in range(2):
        vown[s] = vmsg[y, s] + vnear[0, s] + vnear[1, s] + vnear[2, s]
    v2 = remote(vown.at[1 - c], vcore, sv2.at[0], qv2.at[0], core_peer)
    v2.start()

    def add(i, totals):
        return tuple(t + counts[i * 8 + k] for k, t in enumerate(totals))

    totals = lax.fori_loop(0, 64, add, (jnp.int32(0),) * 8)
    total = sum(totals[1:], totals[0])
    scale = 1.0 / (jnp.zeros((1, 128), jnp.float32) + total.astype(jnp.float32))

    v2.wait()
    for l in range(2):
        vboth[l, c] = vown[c, l, 0:16]
        vboth[l, 1 - c] = vcore[l, 0:16]
        diag_own[l] = vown[c, l, 16:18] + vcore[l, 16:18]
    pl.semaphore_wait(ready.at[1], 2)
    far_first = (8, 7, 9, 6, 10, 5, 11, 4, 12, 3, 13, 2, 14, 1, 15)
    v3 = [
        remote(vboth.at[(z + i) % 2], vfar.at[i - 1], sv3.at[i - 1], qv3.at[i - 1], z_peers[i - 1])
        for i in range(1, 16)
    ]
    e3 = [
        remote(diag_own.at[(z + i) % 2], diag_far.at[i - 1], se3.at[i - 1], qe3.at[i - 1], z_peers[i - 1])
        for i in range(1, 16)
    ]

    def kept(step, side):
        row = (zlo + 4 - step) % 4
        turn = (y - row + 4) % 4
        return (turn < 2) | ((turn == 2) & (row // 2 == side))

    for odd in range(2):

        @pl.when(kept(0, (layer + odd) % 2))
        def _():
            for i in far_first:
                if i % 2 == odd:
                    v3[i - 1].start()

    for i in far_first:
        e3[i - 1].start()

    second = [[[] for _ in range(4)] for _ in range(2)]

    def to_second(t):
        for l in range(2):
            for copy in first[l][t]:
                copy.wait()
            chunk[l, t] = (
                terms[l, where[l], :, pl.ds(quads[t] * 2, 2)] + near[l, t, 0] + near[l, t, 1] + near[l, t, 2]
            )
            for i in (2, 1, 3):
                at = (l * 4 + t) * 3 + i - 1
                copy = remote(
                    chunk.at[l, t, (where[1 - l] + i) % 4],
                    near2.at[l, t, i - 1],
                    s2.at[at],
                    q2.at[at],
                    across[1 - l][i - 1],
                )
                copy.start()
                second[l][t].append(copy)

    def to_planes(t):
        for l in range(2):
            for copy in second[l][t]:
                copy.wait()
            part[l, t] = chunk[l, t, where[1 - l]] + near2[l, t, 0] + near2[l, t, 1] + near2[l, t, 2]
        for r in range(1 if t == 3 else 0, 4):
            lane = (zlo + r) % 4
            target = quads[t] * 4 + lane
            at = (target + 16 - z) % 16 - 1
            remote(
                part.at[lane % 2, t, lane // 2], zrecv.at[at], s3.at[at], q3.at[at], device(x, y, target, c)
            ).start()

    to_second(0)
    to_second(1)
    to_planes(0)
    to_second(2)
    to_planes(1)
    to_second(3)
    to_planes(2)
    to_planes(3)

    for odd in range(2):

        @pl.when(kept(0, (layer + odd) % 2))
        def _():
            for i in range(1, 16):
                if i % 2 == odd:
                    v3[i - 1].wait_send()

    for r in range(4):

        @pl.when(kept(r, layer))
        def _():
            got = vboth[layer] if r == 0 else None
            for i in range(r or 4, 16, 4):
                v3[i - 1].wait_recv()
                got = vfar[i - 1] if got is None else got + vfar[i - 1]
            vpart[(zlo + 4 - r) % 4] = got

    v4 = []
    for d in range(3):
        row = (y + 4 - d) % 4
        v4.append(
            [
                remote(
                    vpart.at[row], vcols.at[y, row, x], sv4.at[d * 15 + k], qv4.at[d * 15 + k], plane_peers[k]
                )
                for k in range(15)
            ]
        )
    for d in range(2):
        row = (y + 4 - d) % 4
        vcols[y, row, x] = vpart[row]
        for copy in v4[d]:
            copy.start()

    @pl.when((y // 2 + layer) % 2 == 1)
    def _():
        row = (y + 2) % 4
        vcols[y, row, x] = vpart[row]
        for copy in v4[2]:
            copy.start()

    got = diag_own[layer]
    for i in range(15):
        e3[i].wait()
        got = got + diag_far[i]
    diag_sum[...] = got
    e4 = [remote(diag_sum, diag_x.at[i], se4.at[i], qe4.at[i], x_peers[i]) for i in range(3)]
    for copy in e4:
        copy.start()

    for i in range(15):
        remote(part.at[0, 0, 0], zrecv.at[i], s3.at[i], q3.at[i], z_peers[i]).wait()
    got = part[layer, 3, zlo // 2]
    for i in range(15):
        got = got + zrecv[i]
    unit[...] = got * scale
    zgath[0] = unit[...]
    fourth = {
        i: remote(unit, zgath.at[k + 1], s4.at[k], q4.at[k], z_peers[i - 1])
        for k, i in enumerate(NEAR_FIRST)
    }
    for i in (8, 6, 10, 4, 12, 2, 14):
        fourth[i].start()
    mine = jnp.where(layer == 0, x * 4 + y, y * 4 + x)
    fifth = []
    straight = []
    for k in range(5):
        i, j = plane_shift[k]
        straight.append(
            remote(
                unit, stack.at[mine, 7], s5.at[70 + k], q5.at[70 + k], device((x + i) % 4, (y + j) % 4, (z + 8) % 16, c)
            )
        )
        straight[k].start()
    for lo, hi in ((0, 1), (1, 3), (3, 5), (5, 7), (7, 8)):
        for i in NEAR_FIRST[max(lo, 1) - 1 : hi - 1]:
            fourth[i].wait_recv()
        for k in range(5 if lo == 7 else 0, 15):
            at = len(fifth)
            fifth.append(
                remote(zgath.at[lo:hi], stack.at[mine, lo:hi], s5.at[at], q5.at[at], plane_peers[k])
            )
            fifth[at].start()
    stack[mine] = zgath[...]

    for k, (i, j) in enumerate(plane_shift):
        v4[0][k].wait()
        v4[1][k].wait()

        @pl.when(((y + 4 - j) % 4 // 2 + layer) % 2 == 1)
        def _():
            v4[2][k].wait_recv()

        @pl.when((y // 2 + layer) % 2 == 1)
        def _():
            v4[2][k].wait_send()

    for a in range(4):
        for b in (a, (a + 1) % 4):
            block = vcols[b, a].reshape(128, 128)
            vfull[128 * a : 128 * a + 128, 128 * b : 128 * b + 128] = block
            if a != b:
                vfull[128 * b : 128 * b + 128, 128 * a : 128 * a + 128] = block.T
    for a in range(2):
        b = a + 2
        block = vcols[a + 2 * (1 - layer), a + 2 * layer].reshape(128, 128)
        turned = block.T
        vfull[128 * a : 128 * a + 128, 128 * b : 128 * b + 128] = jnp.where(layer == 0, block, turned)
        vfull[128 * b : 128 * b + 128, 128 * a : 128 * a + 128] = jnp.where(layer == 0, turned, block)
    row_a = jnp.where(c == 1, (zlo // 2 * 2) * 4 + x, y * 4 + zhi)
    row_b = jnp.where(c == 1, (zlo // 2 * 2 + 1) * 4 + x, y * 4 + zhi)
    rows_in[0:32] = vfull[pl.ds(pl.multiple_of(row_a * 32, 32), 32)]
    rows_in[32:64] = vfull[pl.ds(pl.multiple_of(row_b * 32, 32), 32)]
    loads[5].wait()

    @pl.when(c == 0)
    def _():
        top, low = split(vfull[...])
        other_hi[...] = top
        other_lo[...] = low
        base[...] = 2.0 * rows_in[...]

    @pl.when(c == 1)
    def _():
        right = split(gmat[...])
        top, low = split(three(split(vfull[...]), right))
        other_hi[...] = top
        other_lo[...] = low
        base[...] = 2.0 * three(split(rows_in[...]), right)

    for copy in e4:
        copy.wait()
    second_diag = (diag_sum[...] + diag_x[0] + diag_x[1] + diag_x[2]) * scale

    for copy in fifth + straight:
        copy.wait()
    for i in NEAR_FIRST:
        fourth[i].wait_send()
    for k, i in enumerate((0,) + NEAR_FIRST):
        at = (z + 16 - i) % 16 // 2
        for p in range(16):
            ordered[p, at] = stack[p, k]

    on_diag = lax.broadcasted_iota(jnp.int32, (128, 128), 0) == lax.broadcasted_iota(jnp.int32, (128, 128), 1)
    eye = jnp.where(on_diag, damping, 0.0).astype(jnp.float32)
    for k in range(2):
        both = ordered[2 * k : 2 * k + 2].reshape(128, 128)
        turned = both.T
        at = 256 * k
        full[at : at + 128, at : at + 128] = jnp.where(at_or_above, both, turned) + eye
        lower = jnp.where(at_or_above, turned, both)
        full[at + 128 : at + 256, at + 128 : at + 256] = (
            jnp.where(on_diag, second_diag[k : k + 1, :], lower) + eye
        )
    for k, (i, j) in enumerate(PAIRS):
        block = ordered[4 + 2 * k : 6 + 2 * k].reshape(128, 128)
        full[128 * i : 128 * i + 128, 128 * j : 128 * j + 128] = block
        full[128 * j : 128 * j + 128, 128 * i : 128 * i + 128] = block.T

    def rows_of(plane_lo, core):
        return pl.ds(pl.multiple_of(plane_lo * 128 + x * 32 + core * 16, 16), 16)

    pair_lo = zpair % 4
    fcopies = [
        remote(full.at[rows_of(zlo, 1 - c)], fin.at[layer, c], sf.at[0], qf.at[0], core_peer),
        remote(full.at[rows_of(pair_lo, c)], fin.at[layer, c], sf.at[1], qf.at[1], pair_peer),
        remote(full.at[rows_of(pair_lo, 1 - c)], fin.at[layer, c], sf.at[2], qf.at[2], cross_peer),
    ]
    for copy in fcopies:
        copy.start()
    fin[layer, c] = full[rows_of(zlo, c)]

    half_way = three(split(rows_in[...]), split(full[...]))
    newrows[...] = base[...] - three(split(half_way), (other_hi[...], other_lo[...]))

    rcopy = remote(newrows.at[0:32], partner, sr.at[0], qr.at[0], core_peer)

    @pl.when(c == 0)
    def _():
        rcopy.start()

    targets = [device(x, y, z, 0), device(x, y, zpair, 0), device(x, y, zpair, 1)]
    order = [(layer, 0), (1 - layer, 0), (1 - layer, 1)]
    pcopies = [
        remote(pblock.at[a * 2 + b], pin.at[layer], sp.at[k], qp.at[layer], targets[k])
        for k, (a, b) in enumerate(order)
    ]

    @pl.when(c == 1)
    def _():
        rcopy.wait_recv()
        result = three(split(newrows[...]), split(partner[...]), (((1,), (1,)), ((), ())))
        for k in range(4):
            pblock[k] = result[16 * k : 16 * k + 16]
        pin[layer] = pblock[layer * 2 + 1]
        for copy in pcopies:
            copy.start()

    for copy in fcopies:
        copy.wait()
    for l in range(2):
        for s in range(2):
            keep_slot = jnp.where(owners[l, s] == grp, 1.0, 0.0).astype(jnp.float32)
            slots_out[l, s] = fin[l, s] * keep_slot

    @pl.when(c == 0)
    def _():
        rcopy.wait_send()
        remote(pblock.at[0], pin.at[layer], sp.at[0], qp.at[layer], core_peer).wait_recv()

    @pl.when(c == 1)
    def _():
        for copy in pcopies:
            copy.wait_send()

    remote(pblock.at[0], pin.at[1 - layer], sp.at[0], qp.at[1 - layer], core_peer).wait_recv()
    pre_out[...] = pin[...]


def body(activations, out_grads, inverse_slots, gradient, owners, counts):
    f32, bf16 = jnp.float32, jnp.bfloat16
    whole = pl.BlockSpec(memory_space=pltpu.VMEM)
    vm = lambda *shape: pltpu.VMEM(shape, f32)
    dma = lambda n: pltpu.SemaphoreType.DMA((n,))
    operands = (owners, counts, activations, out_grads, inverse_slots, gradient)
    return pl.pallas_call(
        kernel,
        out_shape=(
            jax.ShapeDtypeStruct((2, 2, 16, 512), f32),
            jax.ShapeDtypeStruct((2, 16, 32), f32),
        ),
        in_specs=[pl.BlockSpec(memory_space=pltpu.HBM)] * 6,
        out_specs=(whole, whole),
        scratch_shapes=[
            pltpu.SMEM((2, 2), jnp.int32),
            pltpu.SMEM((512,), jnp.int32),
            pltpu.VMEM((2, 2, 128, 512), bf16),
            vm(2, 2, 16, 512),
            vm(512, 512),
            vm(2, 512, 128),
            vm(2, 512, 128),
            pltpu.VMEM((2, 512, 256), bf16),
            vm(2, 4, 4, 8, 8, 128),
            vm(2, 4, 3, 4, 2, 8, 128),
            vm(2, 4, 4, 2, 8, 128),
            vm(2, 4, 3, 2, 8, 128),
            vm(2, 4, 2, 8, 128),
            vm(15, 8, 128),
            vm(8, 128),
            vm(8, 8, 128),
            vm(16, 8, 8, 128),
            vm(16, 8, 8, 128),
            vm(512, 512),
            vm(4, 2, 2, 18, 128),
            vm(3, 2, 2, 18, 128),
            vm(2, 2, 18, 128),
            vm(2, 18, 128),
            vm(2, 2, 16, 128),
            vm(15, 2, 16, 128),
            vm(4, 2, 16, 128),
            vm(4, 4, 4, 2, 16, 128),
            vm(512, 512),
            vm(64, 512),
            pltpu.VMEM((512, 512), bf16),
            pltpu.VMEM((512, 512), bf16),
            vm(64, 512),
            vm(2, 2, 128),
            vm(15, 2, 128),
            vm(2, 128),
            vm(3, 2, 128),
            vm(64, 512),
            vm(32, 512),
            vm(4, 16, 32),
            vm(2, 16, 32),
            vm(2, 2, 16, 512),
            dma(6), dma(2), dma(2), dma(24), dma(24), dma(24), dma(24), dma(15), dma(15), dma(7), dma(7),
            dma(75), dma(75),
            dma(3), dma(3), dma(1), dma(1), dma(15), dma(15), dma(45), dma(45), dma(15), dma(15), dma(3), dma(3),
            dma(3), dma(3), dma(1), dma(1), dma(3), dma(2),
            pltpu.SemaphoreType.REGULAR((2,)),
        ],
        compiler_params=pltpu.CompilerParams(
            collective_id=0, has_side_effects=True, vmem_limit_bytes=40 * 1024 * 1024
        ),
    )(*(pltpu.with_memory_space_constraint(a, pltpu.HBM) for a in operands))


def solution(mesh):
    placed = (
        P(None, ("grp", "mem"), None),
        P(None, ("grp", "mem"), None),
        P(None, None, ("grp", "mem"), None),
        P(),
        P(),
        P(),
    )
    return jax.shard_map(
        body,
        mesh=mesh,
        in_specs=placed,
        out_specs=(P(None, None, ("grp", "mem"), None), P(None, "mem", "grp")),
        check_vma=False,
    )
```

```python
import jax
import jax.numpy as jnp
from jax import lax
from jax.experimental import pallas as pl
from jax.experimental.pallas import tpu as pltpu
from jax.sharding import PartitionSpec as P

MESH = pl.DeviceIdType.MESH
damping = 0.1


def device(x, y, z, c):
    return (y * 4 + z // 4, (z % 4) * 8 + x * 2 + c)


def split(a):
    top = a.astype(jnp.bfloat16)
    return top, (a - top.astype(jnp.float32)).astype(jnp.bfloat16)


def three(a, b, dims=(((1,), (0,)), ((), ()))):
    one = lambda p, q: lax.dot_general(p, q, dims, preferred_element_type=jnp.float32)
    return one(a[0], b[0]) + (one(a[0], b[1]) + one(a[1], b[0]))


NEAR_FIRST = (2, 14, 4, 12, 6, 10, 8)
PAIRS = ((0, 1), (0, 2), (0, 3), (1, 2), (1, 3), (2, 3))


def kernel(
    owners_in, counts_in, acts, grads, slots, gradient,
    slots_out, pre_out,
    owners, counts, xin, inv, gmat, xsend, xrecv, xcat, terms, near, chunk, near2, part,
    zrecv, unit, zgath, stack, ordered, full,
    vmsg, vnear, vown, vcore, vboth, vfar, vpart, vcols, vfull, rows_in, other_hi, other_lo, base,
    diag_own, diag_far, diag_sum, diag_x,
    newrows, partner, pblock, pin, fin,
    lsem, xss, xrs, s1, q1, s2, q2, s3, q3, s4, q4, s5, q5,
    sv1, qv1, sv2, qv2, sv3, qv3, sv4, qv4, se3, qe3, se4, qe4, sf, qf, sr, qr, sp, qp, ready,
):
    grp = lax.axis_index("grp")
    mem = lax.axis_index("mem")
    y = grp // 4
    z = (grp % 4) * 4 + mem // 8
    x = (mem // 2) % 4
    c = mem % 2
    zlo = z % 4
    zhi = z // 4
    layer = z % 2
    zpair = z + 1 - 2 * layer

    def remote(src, dst, ssem, rsem, target):
        return pltpu.make_async_remote_copy(
            src_ref=src, dst_ref=dst, send_sem=ssem, recv_sem=rsem, device_id=target, device_id_type=MESH
        )

    def signal(sem, peer):
        pl.semaphore_signal(sem, inc=1, device_id=peer, device_id_type=MESH)

    core_peer = device(x, y, z, 1 - c)
    x_peers = [device((x + i) % 4, y, z, c) for i in range(1, 4)]
    y_peers = [device(x, (y + i) % 4, z, c) for i in range(1, 4)]
    plane_shift = sorted(
        [(i, j) for i in range(4) for j in range(4) if i or j], key=lambda at: -(min(at[0], 4 - at[0]) + min(at[1], 4 - at[1]))
    )
    plane_peers = [device((x + i) % 4, (y + j) % 4, z, c) for i, j in plane_shift]
    z_peers = [device(x, y, (z + i) % 16, c) for i in range(1, 16)]
    pair_peer = device(x, y, zpair, c)
    cross_peer = device(x, y, zpair, 1 - c)
    barrier = pltpu.get_barrier_semaphore()
    close = [core_peer] + x_peers + y_peers + [z_peers[i - 1] for i in (1, 2, 14, 15)]
    for peer in close:
        signal(barrier, peer)

    loads = [
        pltpu.make_async_copy(counts_in, counts, lsem.at[0]),
        pltpu.make_async_copy(acts, xin.at[0], lsem.at[1]),
        pltpu.make_async_copy(grads, xin.at[1], lsem.at[2]),
        pltpu.make_async_copy(owners_in, owners, lsem.at[3]),
        pltpu.make_async_copy(slots, inv, lsem.at[4]),
        pltpu.make_async_copy(gradient.at[layer], gmat, lsem.at[5]),
    ]
    for load in loads:
        load.start()

    for k in range(3):
        loads[k].wait()
    live = counts[grp * 32 + mem]
    keep = lax.broadcasted_iota(jnp.int32, (128, 512), 0) < live
    for l in range(2):
        theirs = jnp.where(keep, xin[1 - c, l].astype(jnp.float32), 0.0)
        xsend[l] = theirs.T
        ours = jnp.where(keep, xin[c, l].astype(jnp.float32), 0.0)
        xcat[l, :, 0:128] = ours.T.astype(jnp.bfloat16)
        for s, values in ((1 - c, theirs), (c, ours)):
            squares = jnp.sum(values * values, axis=0, keepdims=True)
            for k in range(4):
                vmsg[k, s, l, 16:17] = squares[:, 128:256]
                vmsg[k, s, l, 17:18] = squares[:, 384:512]
    loads[3].wait()
    loads[4].wait()
    for l in range(2):
        for s in range(2):
            mask = jnp.where(owners[l, s] == grp, 1.0, 0.0).astype(jnp.float32)
            for k in range(4):
                vmsg[k, s, l, 0:16] = inv[l, s, :, 128 * k : 128 * k + 128] * mask

    pl.semaphore_wait(barrier, len(close))

    xcopies = [remote(xsend.at[l], xrecv.at[l], xss.at[l], xrs.at[l], core_peer) for l in range(2)]
    for copy in xcopies:
        copy.start()
    signal(ready.at[0], z_peers[1])
    signal(ready.at[0], z_peers[13])
    v1 = [
        remote(vmsg.at[(y + i) % 4], vnear.at[i - 1], sv1.at[i - 1], qv1.at[i - 1], y_peers[i - 1])
        for i in range(1, 4)
    ]

    for copy in v1:
        copy.start()
    where = (x, y)
    across = (x_peers, y_peers)
    at_or_above = lax.broadcasted_iota(jnp.int32, (128, 128), 0) <= lax.broadcasted_iota(
        jnp.int32, (128, 128), 1
    )
    turn_to = jnp.where(zlo < 2, 1, 3)
    quads = [(zhi + 2) % 4, (zhi + turn_to) % 4, (zhi + 4 - turn_to) % 4, zhi]
    first = [[[] for _ in range(4)] for _ in range(2)]
    for l in range(2):
        xcopies[l].wait()
        xcat[l, :, 128:256] = xrecv[l].astype(jnp.bfloat16)
        right = [
            lax.dot_general(
                xcat[l, 0 : 256 + 256 * k],
                xcat[l, 256 * k : 256 * k + 256],
                (((1,), (1,)), ((), ())),
                preferred_element_type=jnp.float32,
            )
            for k in range(2)
        ]

        def pair(i, j):
            return right[j // 2][128 * i : 128 * i + 128, 128 * (j % 2) : 128 * (j % 2) + 128]

        terms[l, 0, 0:2] = jnp.where(at_or_above, pair(0, 0), pair(1, 1)).reshape(2, 8, 8, 128)
        terms[l, 0, 2:4] = jnp.where(at_or_above, pair(2, 2), pair(3, 3)).reshape(2, 8, 8, 128)
        for k, (i, j) in enumerate(PAIRS):
            b = k + 2
            terms[l, b // 2, b % 2 * 2 : b % 2 * 2 + 2] = pair(i, j).reshape(2, 8, 8, 128)
        for t in range(4):
            for i in (2, 1, 3):
                at = (l * 4 + t) * 3 + i - 1
                copy = remote(
                    terms.at[l, (where[l] + i) % 4, :, pl.ds(quads[t] * 2, 2)],
                    near.at[l, t, i - 1],
                    s1.at[at],
                    q1.at[at],
                    across[l][i - 1],
                )
                copy.start()
                first[l][t].append(copy)

    pl.semaphore_wait(ready.at[0], 2)
    signal(ready.at[1], z_peers[3])
    signal(ready.at[1], z_peers[11])

    for copy in v1:
        copy.wait()
    for s in range(2):
        vown[s] = vmsg[y, s] + vnear[0, s] + vnear[1, s] + vnear[2, s]
    v2 = remote(vown.at[1 - c], vcore, sv2.at[0], qv2.at[0], core_peer)
    v2.start()

    def add(i, totals):
        return tuple(t + counts[i * 8 + k] for k, t in enumerate(totals))

    totals = lax.fori_loop(0, 64, add, (jnp.int32(0),) * 8)
    total = sum(totals[1:], totals[0])
    scale = 1.0 / (jnp.zeros((1, 128), jnp.float32) + total.astype(jnp.float32))

    v2.wait()
    for l in range(2):
        vboth[l, c] = vown[c, l, 0:16]
        vboth[l, 1 - c] = vcore[l, 0:16]
        diag_own[l] = vown[c, l, 16:18] + vcore[l, 16:18]
    pl.semaphore_wait(ready.at[1], 2)
    far_first = (8, 7, 9, 6, 10, 5, 11, 4, 12, 3, 13, 2, 14, 1, 15)
    v3 = [
        remote(vboth.at[(z + i) % 2], vfar.at[i - 1], sv3.at[i - 1], qv3.at[i - 1], z_peers[i - 1])
        for i in range(1, 16)
    ]
    e3 = [
        remote(diag_own.at[(z + i) % 2], diag_far.at[i - 1], se3.at[i - 1], qe3.at[i - 1], z_peers[i - 1])
        for i in range(1, 16)
    ]

    def kept(step, side, column=y):
        row = (zlo + 4 - step) % 4
        turn = (column - row + 4) % 4
        return (turn < 2) | ((turn == 2) & (row // 2 == side))

    steps = (0, 1, 3, 2)
    for r in steps:

        @pl.when(kept(0, (layer + r) % 2))
        def _():
            for i in far_first:
                if i % 4 == r:
                    v3[i - 1].start()

    for i in far_first:
        e3[i - 1].start()

    second = [[[] for _ in range(4)] for _ in range(2)]

    def to_second(t):
        for l in range(2):
            for copy in first[l][t]:
                copy.wait()
            chunk[l, t] = (
                terms[l, where[l], :, pl.ds(quads[t] * 2, 2)] + near[l, t, 0] + near[l, t, 1] + near[l, t, 2]
            )
            for i in (2, 1, 3):
                at = (l * 4 + t) * 3 + i - 1
                copy = remote(
                    chunk.at[l, t, (where[1 - l] + i) % 4],
                    near2.at[l, t, i - 1],
                    s2.at[at],
                    q2.at[at],
                    across[1 - l][i - 1],
                )
                copy.start()
                second[l][t].append(copy)

    def to_planes(t):
        for l in range(2):
            for copy in second[l][t]:
                copy.wait()
            part[l, t] = chunk[l, t, where[1 - l]] + near2[l, t, 0] + near2[l, t, 1] + near2[l, t, 2]
        for r in range(1 if t == 3 else 0, 4):
            lane = (zlo + r) % 4
            target = quads[t] * 4 + lane
            at = (target + 16 - z) % 16 - 1
            remote(
                part.at[lane % 2, t, lane // 2], zrecv.at[at], s3.at[at], q3.at[at], device(x, y, target, c)
            ).start()

    to_second(0)
    to_second(1)
    to_planes(0)
    to_second(2)
    to_planes(1)
    to_second(3)
    to_planes(2)
    to_planes(3)

    v4 = [
        [
            remote(
                vpart.at[(zlo + 4 - r) % 4],
                vcols.at[y, (zlo + 4 - r) % 4, x],
                sv4.at[r * 15 + k],
                qv4.at[r * 15 + k],
                plane_peers[k],
            )
            for k in range(15)
        ]
        for r in range(4)
    ]
    for r in steps:

        @pl.when(kept(r, layer))
        def _():
            got = vboth[layer] if r == 0 else None
            for i in range(r or 4, 16, 4):
                v3[i - 1].wait_recv()
                got = vfar[i - 1] if got is None else got + vfar[i - 1]
            row = (zlo + 4 - r) % 4
            vpart[row] = got
            vcols[y, row, x] = got
            for copy in v4[r]:
                copy.start()

    for odd in range(2):

        @pl.when(kept(0, (layer + odd) % 2))
        def _():
            for i in range(1, 16):
                if i % 2 == odd:
                    v3[i - 1].wait_send()

    got = diag_own[layer]
    for i in range(15):
        e3[i].wait()
        got = got + diag_far[i]
    diag_sum[...] = got
    e4 = [remote(diag_sum, diag_x.at[i], se4.at[i], qe4.at[i], x_peers[i]) for i in range(3)]
    for copy in e4:
        copy.start()

    for i in range(15):
        remote(part.at[0, 0, 0], zrecv.at[i], s3.at[i], q3.at[i], z_peers[i]).wait()
    got = part[layer, 3, zlo // 2]
    for i in range(15):
        got = got + zrecv[i]
    unit[...] = got * scale
    zgath[0] = unit[...]
    fourth = {
        i: remote(unit, zgath.at[k + 1], s4.at[k], q4.at[k], z_peers[i - 1])
        for k, i in enumerate(NEAR_FIRST)
    }
    for i in (8, 6, 10, 4, 12, 2, 14):
        fourth[i].start()
    mine = jnp.where(layer == 0, x * 4 + y, y * 4 + x)
    fifth = []
    straight = []
    for k in range(5):
        i, j = plane_shift[k]
        straight.append(
            remote(
                unit, stack.at[mine, 7], s5.at[70 + k], q5.at[70 + k], device((x + i) % 4, (y + j) % 4, (z + 8) % 16, c)
            )
        )
        straight[k].start()
    for lo, hi in ((0, 1), (1, 3), (3, 5), (5, 7), (7, 8)):
        for i in NEAR_FIRST[max(lo, 1) - 1 : hi - 1]:
            fourth[i].wait_recv()
        for k in range(5 if lo == 7 else 0, 15):
            at = len(fifth)
            fifth.append(
                remote(zgath.at[lo:hi], stack.at[mine, lo:hi], s5.at[at], q5.at[at], plane_peers[k])
            )
            fifth[at].start()
    stack[mine] = zgath[...]

    for r in range(4):
        for back in range(4):

            @pl.when(kept(r, layer, (y + 4 - back) % 4))
            def _():
                for k, (i, j) in enumerate(plane_shift):
                    if j == back:
                        v4[r][k].wait_recv()

        @pl.when(kept(r, layer))
        def _():
            for copy in v4[r]:
                copy.wait_send()

    for a in range(4):
        for b in (a, (a + 1) % 4):
            block = vcols[b, a].reshape(128, 128)
            vfull[128 * a : 128 * a + 128, 128 * b : 128 * b + 128] = block
            if a != b:
                vfull[128 * b : 128 * b + 128, 128 * a : 128 * a + 128] = block.T
    for a in range(2):
        b = a + 2
        block = vcols[a + 2 * (1 - layer), a + 2 * layer].reshape(128, 128)
        turned = block.T
        vfull[128 * a : 128 * a + 128, 128 * b : 128 * b + 128] = jnp.where(layer == 0, block, turned)
        vfull[128 * b : 128 * b + 128, 128 * a : 128 * a + 128] = jnp.where(layer == 0, turned, block)
    row_a = jnp.where(c == 1, (zlo // 2 * 2) * 4 + x, y * 4 + zhi)
    row_b = jnp.where(c == 1, (zlo // 2 * 2 + 1) * 4 + x, y * 4 + zhi)
    rows_in[0:32] = vfull[pl.ds(pl.multiple_of(row_a * 32, 32), 32)]
    rows_in[32:64] = vfull[pl.ds(pl.multiple_of(row_b * 32, 32), 32)]
    loads[5].wait()

    @pl.when(c == 0)
    def _():
        top, low = split(vfull[...])
        other_hi[...] = top
        other_lo[...] = low
        base[...] = 2.0 * rows_in[...]

    @pl.when(c == 1)
    def _():
        right = split(gmat[...])
        top, low = split(three(split(vfull[...]), right))
        other_hi[...] = top
        other_lo[...] = low
        base[...] = 2.0 * three(split(rows_in[...]), right)

    for copy in e4:
        copy.wait()
    second_diag = (diag_sum[...] + diag_x[0] + diag_x[1] + diag_x[2]) * scale

    for copy in fifth + straight:
        copy.wait()
    for i in NEAR_FIRST:
        fourth[i].wait_send()
    for k, i in enumerate((0,) + NEAR_FIRST):
        at = (z + 16 - i) % 16 // 2
        for p in range(16):
            ordered[p, at] = stack[p, k]

    on_diag = lax.broadcasted_iota(jnp.int32, (128, 128), 0) == lax.broadcasted_iota(jnp.int32, (128, 128), 1)
    eye = jnp.where(on_diag, damping, 0.0).astype(jnp.float32)
    for k in range(2):
        both = ordered[2 * k : 2 * k + 2].reshape(128, 128)
        turned = both.T
        at = 256 * k
        full[at : at + 128, at : at + 128] = jnp.where(at_or_above, both, turned) + eye
        lower = jnp.where(at_or_above, turned, both)
        full[at + 128 : at + 256, at + 128 : at + 256] = (
            jnp.where(on_diag, second_diag[k : k + 1, :], lower) + eye
        )
    for k, (i, j) in enumerate(PAIRS):
        block = ordered[4 + 2 * k : 6 + 2 * k].reshape(128, 128)
        full[128 * i : 128 * i + 128, 128 * j : 128 * j + 128] = block
        full[128 * j : 128 * j + 128, 128 * i : 128 * i + 128] = block.T

    def rows_of(plane_lo, core):
        return pl.ds(pl.multiple_of(plane_lo * 128 + x * 32 + core * 16, 16), 16)

    pair_lo = zpair % 4
    fcopies = [
        remote(full.at[rows_of(zlo, 1 - c)], fin.at[layer, c], sf.at[0], qf.at[0], core_peer),
        remote(full.at[rows_of(pair_lo, c)], fin.at[layer, c], sf.at[1], qf.at[1], pair_peer),
        remote(full.at[rows_of(pair_lo, 1 - c)], fin.at[layer, c], sf.at[2], qf.at[2], cross_peer),
    ]
    for copy in fcopies:
        copy.start()
    fin[layer, c] = full[rows_of(zlo, c)]

    half_way = three(split(rows_in[...]), split(full[...]))
    newrows[...] = base[...] - three(split(half_way), (other_hi[...], other_lo[...]))

    rcopy = remote(newrows.at[0:32], partner, sr.at[0], qr.at[0], core_peer)

    @pl.when(c == 0)
    def _():
        rcopy.start()

    targets = [device(x, y, z, 0), device(x, y, zpair, 0), device(x, y, zpair, 1)]
    order = [(layer, 0), (1 - layer, 0), (1 - layer, 1)]
    pcopies = [
        remote(pblock.at[a * 2 + b], pin.at[layer], sp.at[k], qp.at[layer], targets[k])
        for k, (a, b) in enumerate(order)
    ]

    @pl.when(c == 1)
    def _():
        rcopy.wait_recv()
        result = three(split(newrows[...]), split(partner[...]), (((1,), (1,)), ((), ())))
        for k in range(4):
            pblock[k] = result[16 * k : 16 * k + 16]
        pin[layer] = pblock[layer * 2 + 1]
        for copy in pcopies:
            copy.start()

    for copy in fcopies:
        copy.wait()
    for l in range(2):
        for s in range(2):
            keep_slot = jnp.where(owners[l, s] == grp, 1.0, 0.0).astype(jnp.float32)
            slots_out[l, s] = fin[l, s] * keep_slot

    @pl.when(c == 0)
    def _():
        rcopy.wait_send()
        remote(pblock.at[0], pin.at[layer], sp.at[0], qp.at[layer], core_peer).wait_recv()

    @pl.when(c == 1)
    def _():
        for copy in pcopies:
            copy.wait_send()

    remote(pblock.at[0], pin.at[1 - layer], sp.at[0], qp.at[1 - layer], core_peer).wait_recv()
    pre_out[...] = pin[...]


def body(activations, out_grads, inverse_slots, gradient, owners, counts):
    f32, bf16 = jnp.float32, jnp.bfloat16
    whole = pl.BlockSpec(memory_space=pltpu.VMEM)
    vm = lambda *shape: pltpu.VMEM(shape, f32)
    dma = lambda n: pltpu.SemaphoreType.DMA((n,))
    operands = (owners, counts, activations, out_grads, inverse_slots, gradient)
    return pl.pallas_call(
        kernel,
        out_shape=(
            jax.ShapeDtypeStruct((2, 2, 16, 512), f32),
            jax.ShapeDtypeStruct((2, 16, 32), f32),
        ),
        in_specs=[pl.BlockSpec(memory_space=pltpu.HBM)] * 6,
        out_specs=(whole, whole),
        scratch_shapes=[
            pltpu.SMEM((2, 2), jnp.int32),
            pltpu.SMEM((512,), jnp.int32),
            pltpu.VMEM((2, 2, 128, 512), bf16),
            vm(2, 2, 16, 512),
            vm(512, 512),
            vm(2, 512, 128),
            vm(2, 512, 128),
            pltpu.VMEM((2, 512, 256), bf16),
            vm(2, 4, 4, 8, 8, 128),
            vm(2, 4, 3, 4, 2, 8, 128),
            vm(2, 4, 4, 2, 8, 128),
            vm(2, 4, 3, 2, 8, 128),
            vm(2, 4, 2, 8, 128),
            vm(15, 8, 128),
            vm(8, 128),
            vm(8, 8, 128),
            vm(16, 8, 8, 128),
            vm(16, 8, 8, 128),
            vm(512, 512),
            vm(4, 2, 2, 18, 128),
            vm(3, 2, 2, 18, 128),
            vm(2, 2, 18, 128),
            vm(2, 18, 128),
            vm(2, 2, 16, 128),
            vm(15, 2, 16, 128),
            vm(4, 2, 16, 128),
            vm(4, 4, 4, 2, 16, 128),
            vm(512, 512),
            vm(64, 512),
            pltpu.VMEM((512, 512), bf16),
            pltpu.VMEM((512, 512), bf16),
            vm(64, 512),
            vm(2, 2, 128),
            vm(15, 2, 128),
            vm(2, 128),
            vm(3, 2, 128),
            vm(64, 512),
            vm(32, 512),
            vm(4, 16, 32),
            vm(2, 16, 32),
            vm(2, 2, 16, 512),
            dma(6), dma(2), dma(2), dma(24), dma(24), dma(24), dma(24), dma(15), dma(15), dma(7), dma(7),
            dma(75), dma(75),
            dma(3), dma(3), dma(1), dma(1), dma(15), dma(15), dma(60), dma(60), dma(15), dma(15), dma(3), dma(3),
            dma(3), dma(3), dma(1), dma(1), dma(3), dma(2),
            pltpu.SemaphoreType.REGULAR((2,)),
        ],
        compiler_params=pltpu.CompilerParams(
            collective_id=0, has_side_effects=True, vmem_limit_bytes=40 * 1024 * 1024
        ),
    )(*(pltpu.with_memory_space_constraint(a, pltpu.HBM) for a in operands))


def solution(mesh):
    placed = (
        P(None, ("grp", "mem"), None),
        P(None, ("grp", "mem"), None),
        P(None, None, ("grp", "mem"), None),
        P(),
        P(),
        P(),
    )
    return jax.shard_map(
        body,
        mesh=mesh,
        in_specs=placed,
        out_specs=(P(None, None, ("grp", "mem"), None), P(None, "mem", "grp")),
        check_vma=False,
    )
```

```python
import jax
import jax.numpy as jnp
from jax import lax
from jax.experimental import pallas as pl
from jax.experimental.pallas import tpu as pltpu
from jax.sharding import PartitionSpec as P

MESH = pl.DeviceIdType.MESH
damping = 0.1


def device(x, y, z, c):
    return (y * 4 + z // 4, (z % 4) * 8 + x * 2 + c)


def split(a):
    top = a.astype(jnp.bfloat16)
    return top, (a - top.astype(jnp.float32)).astype(jnp.bfloat16)


def three(a, b, dims=(((1,), (0,)), ((), ()))):
    one = lambda p, q: lax.dot_general(p, q, dims, preferred_element_type=jnp.float32)
    return one(a[0], b[0]) + (one(a[0], b[1]) + one(a[1], b[0]))


NEAR_FIRST = (2, 14, 4, 12, 6, 10, 8)
PAIRS = ((0, 1), (0, 2), (0, 3), (1, 2), (1, 3), (2, 3))


def kernel(
    owners_in, counts_in, acts, grads, slots, gradient,
    slots_out, pre_out,
    owners, counts, xin, inv, gmat, xsend, xrecv, xcat, terms, near, chunk, near2, part,
    zrecv, unit, zgath, stack, ordered, full,
    vmsg, vnear, vown, vcore, vboth, vfar, vpart, vcols, vfull, rows_in, other_hi, other_lo, base,
    diag_own, diag_far, diag_sum, diag_x,
    newrows, partner, pblock, pin, fin,
    lsem, xss, xrs, s1, q1, s2, q2, s3, q3, s4, q4, s5, q5,
    sv1, qv1, sv2, qv2, sv3, qv3, sv4, qv4, se3, qe3, se4, qe4, sf, qf, sr, qr, sp, qp, ready,
):
    grp = lax.axis_index("grp")
    mem = lax.axis_index("mem")
    y = grp // 4
    z = (grp % 4) * 4 + mem // 8
    x = (mem // 2) % 4
    c = mem % 2
    zlo = z % 4
    zhi = z // 4
    layer = z % 2
    zpair = z + 1 - 2 * layer

    def remote(src, dst, ssem, rsem, target):
        return pltpu.make_async_remote_copy(
            src_ref=src, dst_ref=dst, send_sem=ssem, recv_sem=rsem, device_id=target, device_id_type=MESH
        )

    def signal(sem, peer):
        pl.semaphore_signal(sem, inc=1, device_id=peer, device_id_type=MESH)

    core_peer = device(x, y, z, 1 - c)
    x_peers = [device((x + i) % 4, y, z, c) for i in range(1, 4)]
    y_peers = [device(x, (y + i) % 4, z, c) for i in range(1, 4)]
    plane_shift = sorted(
        [(i, j) for i in range(4) for j in range(4) if i or j], key=lambda at: -(min(at[0], 4 - at[0]) + min(at[1], 4 - at[1]))
    )
    plane_peers = [device((x + i) % 4, (y + j) % 4, z, c) for i, j in plane_shift]
    z_peers = [device(x, y, (z + i) % 16, c) for i in range(1, 16)]
    pair_peer = device(x, y, zpair, c)
    cross_peer = device(x, y, zpair, 1 - c)
    barrier = pltpu.get_barrier_semaphore()
    close = [core_peer] + x_peers + y_peers + [z_peers[i - 1] for i in (1, 2, 14, 15)]
    for peer in close:
        signal(barrier, peer)

    loads = [
        pltpu.make_async_copy(counts_in, counts, lsem.at[0]),
        pltpu.make_async_copy(acts, xin.at[0], lsem.at[1]),
        pltpu.make_async_copy(grads, xin.at[1], lsem.at[2]),
        pltpu.make_async_copy(owners_in, owners, lsem.at[3]),
        pltpu.make_async_copy(slots, inv, lsem.at[4]),
        pltpu.make_async_copy(gradient.at[layer], gmat, lsem.at[5]),
    ]
    for load in loads:
        load.start()

    for k in range(3):
        loads[k].wait()
    live = counts[grp * 32 + mem]
    keep = lax.broadcasted_iota(jnp.int32, (128, 512), 0) < live
    for l in range(2):
        theirs = jnp.where(keep, xin[1 - c, l].astype(jnp.float32), 0.0)
        xsend[l] = theirs.T
        ours = jnp.where(keep, xin[c, l].astype(jnp.float32), 0.0)
        xcat[l, :, 0:128] = ours.T.astype(jnp.bfloat16)
        for s, values in ((1 - c, theirs), (c, ours)):
            squares = jnp.sum(values * values, axis=0, keepdims=True)
            for k in range(4):
                vmsg[k, s, l, 16:17] = squares[:, 128:256]
                vmsg[k, s, l, 17:18] = squares[:, 384:512]
    loads[3].wait()
    loads[4].wait()
    for l in range(2):
        for s in range(2):
            mask = jnp.where(owners[l, s] == grp, 1.0, 0.0).astype(jnp.float32)
            for k in range(4):
                vmsg[k, s, l, 0:16] = inv[l, s, :, 128 * k : 128 * k + 128] * mask

    pl.semaphore_wait(barrier, len(close))

    xcopies = [remote(xsend.at[l], xrecv.at[l], xss.at[l], xrs.at[l], core_peer) for l in range(2)]
    for copy in xcopies:
        copy.start()
    signal(ready.at[0], z_peers[1])
    signal(ready.at[0], z_peers[13])
    v1 = [
        remote(vmsg.at[(y + i) % 4], vnear.at[i - 1], sv1.at[i - 1], qv1.at[i - 1], y_peers[i - 1])
        for i in range(1, 4)
    ]

    for copy in v1:
        copy.start()
    where = (x, y)
    across = (x_peers, y_peers)
    at_or_above = lax.broadcasted_iota(jnp.int32, (128, 128), 0) <= lax.broadcasted_iota(
        jnp.int32, (128, 128), 1
    )
    turn_to = jnp.where(zlo < 2, 1, 3)
    quads = [(zhi + 2) % 4, (zhi + turn_to) % 4, (zhi + 4 - turn_to) % 4, zhi]
    first = [[[] for _ in range(4)] for _ in range(2)]
    for l in range(2):
        xcopies[l].wait()
        xcat[l, :, 128:256] = xrecv[l].astype(jnp.bfloat16)
        right = [
            lax.dot_general(
                xcat[l, 0 : 256 + 256 * k],
                xcat[l, 256 * k : 256 * k + 256],
                (((1,), (1,)), ((), ())),
                preferred_element_type=jnp.float32,
            )
            for k in range(2)
        ]

        def pair(i, j):
            return right[j // 2][128 * i : 128 * i + 128, 128 * (j % 2) : 128 * (j % 2) + 128]

        terms[l, 0, 0:2] = jnp.where(at_or_above, pair(0, 0), pair(1, 1)).reshape(2, 8, 8, 128)
        terms[l, 0, 2:4] = jnp.where(at_or_above, pair(2, 2), pair(3, 3)).reshape(2, 8, 8, 128)
        for k, (i, j) in enumerate(PAIRS):
            b = k + 2
            terms[l, b // 2, b % 2 * 2 : b % 2 * 2 + 2] = pair(i, j).reshape(2, 8, 8, 128)
        for t in range(4):
            for i in (2, 1, 3):
                at = (l * 4 + t) * 3 + i - 1
                copy = remote(
                    terms.at[l, (where[l] + i) % 4, :, pl.ds(quads[t] * 2, 2)],
                    near.at[l, t, i - 1],
                    s1.at[at],
                    q1.at[at],
                    across[l][i - 1],
                )
                copy.start()
                first[l][t].append(copy)
        if l == 0:
            pl.semaphore_wait(ready.at[0], 2)
            signal(ready.at[1], z_peers[3])
            signal(ready.at[1], z_peers[11])

    for copy in v1:
        copy.wait()
    for s in range(2):
        vown[s] = vmsg[y, s] + vnear[0, s] + vnear[1, s] + vnear[2, s]
    v2 = remote(vown.at[1 - c], vcore, sv2.at[0], qv2.at[0], core_peer)
    v2.start()

    def add(i, totals):
        return tuple(t + counts[i * 8 + k] for k, t in enumerate(totals))

    totals = lax.fori_loop(0, 64, add, (jnp.int32(0),) * 8)
    total = sum(totals[1:], totals[0])
    scale = 1.0 / (jnp.zeros((1, 128), jnp.float32) + total.astype(jnp.float32))

    v2.wait()
    for l in range(2):
        vboth[l, c] = vown[c, l, 0:16]
        vboth[l, 1 - c] = vcore[l, 0:16]
        diag_own[l] = vown[c, l, 16:18] + vcore[l, 16:18]
    pl.semaphore_wait(ready.at[1], 2)
    far_first = (8, 7, 9, 6, 10, 5, 11, 4, 12, 3, 13, 2, 14, 1, 15)
    v3 = [
        remote(vboth.at[(z + i) % 2], vfar.at[i - 1], sv3.at[i - 1], qv3.at[i - 1], z_peers[i - 1])
        for i in range(1, 16)
    ]
    e3 = [
        remote(diag_own.at[(z + i) % 2], diag_far.at[i - 1], se3.at[i - 1], qe3.at[i - 1], z_peers[i - 1])
        for i in range(1, 16)
    ]

    def kept(step, side, column=y):
        row = (zlo + 4 - step) % 4
        turn = (column - row + 4) % 4
        return (turn < 2) | ((turn == 2) & (row // 2 == side))

    steps = (0, 1, 3, 2)
    for r in steps:

        @pl.when(kept(0, (layer + r) % 2))
        def _():
            for i in far_first:
                if i % 4 == r:
                    v3[i - 1].start()

    for i in far_first:
        e3[i - 1].start()

    second = [[[] for _ in range(4)] for _ in range(2)]

    def to_second(t):
        for l in range(2):
            for copy in first[l][t]:
                copy.wait()
            chunk[l, t] = (
                terms[l, where[l], :, pl.ds(quads[t] * 2, 2)] + near[l, t, 0] + near[l, t, 1] + near[l, t, 2]
            )
            for i in (2, 1, 3):
                at = (l * 4 + t) * 3 + i - 1
                copy = remote(
                    chunk.at[l, t, (where[1 - l] + i) % 4],
                    near2.at[l, t, i - 1],
                    s2.at[at],
                    q2.at[at],
                    across[1 - l][i - 1],
                )
                copy.start()
                second[l][t].append(copy)

    def to_planes(t):
        for l in range(2):
            for copy in second[l][t]:
                copy.wait()
            part[l, t] = chunk[l, t, where[1 - l]] + near2[l, t, 0] + near2[l, t, 1] + near2[l, t, 2]
        for r in range(1 if t == 3 else 0, 4):
            lane = (zlo + r) % 4
            target = quads[t] * 4 + lane
            at = (target + 16 - z) % 16 - 1
            remote(
                part.at[lane % 2, t, lane // 2], zrecv.at[at], s3.at[at], q3.at[at], device(x, y, target, c)
            ).start()

    to_second(0)
    to_second(1)
    to_planes(0)
    to_second(2)
    to_planes(1)
    to_second(3)
    to_planes(2)
    to_planes(3)

    v4 = [
        [
            remote(
                vpart.at[(zlo + 4 - r) % 4],
                vcols.at[y, (zlo + 4 - r) % 4, x],
                sv4.at[r * 15 + k],
                qv4.at[r * 15 + k],
                plane_peers[k],
            )
            for k in range(15)
        ]
        for r in range(4)
    ]
    for r in steps:

        @pl.when(kept(r, layer))
        def _():
            got = vboth[layer] if r == 0 else None
            for i in range(r or 4, 16, 4):
                v3[i - 1].wait_recv()
                got = vfar[i - 1] if got is None else got + vfar[i - 1]
            row = (zlo + 4 - r) % 4
            vpart[row] = got
            vcols[y, row, x] = got
            for copy in v4[r]:
                copy.start()

    for odd in range(2):

        @pl.when(kept(0, (layer + odd) % 2))
        def _():
            for i in range(1, 16):
                if i % 2 == odd:
                    v3[i - 1].wait_send()

    got = diag_own[layer]
    for i in range(15):
        e3[i].wait()
        got = got + diag_far[i]
    diag_sum[...] = got
    e4 = [remote(diag_sum, diag_x.at[i], se4.at[i], qe4.at[i], x_peers[i]) for i in range(3)]
    for copy in e4:
        copy.start()

    for i in range(15):
        remote(part.at[0, 0, 0], zrecv.at[i], s3.at[i], q3.at[i], z_peers[i]).wait()
    got = part[layer, 3, zlo // 2]
    for i in range(15):
        got = got + zrecv[i]
    unit[...] = got * scale
    zgath[0] = unit[...]
    fourth = {
        i: remote(unit, zgath.at[k + 1], s4.at[k], q4.at[k], z_peers[i - 1])
        for k, i in enumerate(NEAR_FIRST)
    }
    for i in (8, 6, 10, 4, 12, 2, 14):
        fourth[i].start()
    mine = jnp.where(layer == 0, x * 4 + y, y * 4 + x)
    fifth = []
    straight = []
    for k in range(5):
        i, j = plane_shift[k]
        straight.append(
            remote(
                unit, stack.at[mine, 7], s5.at[70 + k], q5.at[70 + k], device((x + i) % 4, (y + j) % 4, (z + 8) % 16, c)
            )
        )
        straight[k].start()
    for lo, hi in ((0, 1), (1, 3), (3, 5), (5, 7), (7, 8)):
        for i in NEAR_FIRST[max(lo, 1) - 1 : hi - 1]:
            fourth[i].wait_recv()
        for k in range(5 if lo == 7 else 0, 15):
            at = len(fifth)
            fifth.append(
                remote(zgath.at[lo:hi], stack.at[mine, lo:hi], s5.at[at], q5.at[at], plane_peers[k])
            )
            fifth[at].start()
    stack[mine] = zgath[...]

    for r in range(4):
        for back in range(4):

            @pl.when(kept(r, layer, (y + 4 - back) % 4))
            def _():
                for k, (i, j) in enumerate(plane_shift):
                    if j == back:
                        v4[r][k].wait_recv()

        @pl.when(kept(r, layer))
        def _():
            for copy in v4[r]:
                copy.wait_send()

    for a in range(4):
        for b in (a, (a + 1) % 4):
            block = vcols[b, a].reshape(128, 128)
            vfull[128 * a : 128 * a + 128, 128 * b : 128 * b + 128] = block
            if a != b:
                vfull[128 * b : 128 * b + 128, 128 * a : 128 * a + 128] = block.T
    for a in range(2):
        b = a + 2
        block = vcols[a + 2 * (1 - layer), a + 2 * layer].reshape(128, 128)
        turned = block.T
        vfull[128 * a : 128 * a + 128, 128 * b : 128 * b + 128] = jnp.where(layer == 0, block, turned)
        vfull[128 * b : 128 * b + 128, 128 * a : 128 * a + 128] = jnp.where(layer == 0, turned, block)
    row_a = jnp.where(c == 1, (zlo // 2 * 2) * 4 + x, y * 4 + zhi)
    row_b = jnp.where(c == 1, (zlo // 2 * 2 + 1) * 4 + x, y * 4 + zhi)
    rows_in[0:32] = vfull[pl.ds(pl.multiple_of(row_a * 32, 32), 32)]
    rows_in[32:64] = vfull[pl.ds(pl.multiple_of(row_b * 32, 32), 32)]
    loads[5].wait()

    @pl.when(c == 0)
    def _():
        top, low = split(vfull[...])
        other_hi[...] = top
        other_lo[...] = low
        base[...] = 2.0 * rows_in[...]

    @pl.when(c == 1)
    def _():
        right = split(gmat[...])
        top, low = split(three(split(vfull[...]), right))
        other_hi[...] = top
        other_lo[...] = low
        base[...] = 2.0 * three(split(rows_in[...]), right)

    for copy in e4:
        copy.wait()
    second_diag = (diag_sum[...] + diag_x[0] + diag_x[1] + diag_x[2]) * scale

    for copy in fifth + straight:
        copy.wait()
    for i in NEAR_FIRST:
        fourth[i].wait_send()
    for k, i in enumerate((0,) + NEAR_FIRST):
        at = (z + 16 - i) % 16 // 2
        for p in range(16):
            ordered[p, at] = stack[p, k]

    on_diag = lax.broadcasted_iota(jnp.int32, (128, 128), 0) == lax.broadcasted_iota(jnp.int32, (128, 128), 1)
    eye = jnp.where(on_diag, damping, 0.0).astype(jnp.float32)
    for k in range(2):
        both = ordered[2 * k : 2 * k + 2].reshape(128, 128)
        turned = both.T
        at = 256 * k
        full[at : at + 128, at : at + 128] = jnp.where(at_or_above, both, turned) + eye
        lower = jnp.where(at_or_above, turned, both)
        full[at + 128 : at + 256, at + 128 : at + 256] = (
            jnp.where(on_diag, second_diag[k : k + 1, :], lower) + eye
        )
    for k, (i, j) in enumerate(PAIRS):
        block = ordered[4 + 2 * k : 6 + 2 * k].reshape(128, 128)
        full[128 * i : 128 * i + 128, 128 * j : 128 * j + 128] = block
        full[128 * j : 128 * j + 128, 128 * i : 128 * i + 128] = block.T

    def rows_of(plane_lo, core):
        return pl.ds(pl.multiple_of(plane_lo * 128 + x * 32 + core * 16, 16), 16)

    pair_lo = zpair % 4
    fcopies = [
        remote(full.at[rows_of(zlo, 1 - c)], fin.at[layer, c], sf.at[0], qf.at[0], core_peer),
        remote(full.at[rows_of(pair_lo, c)], fin.at[layer, c], sf.at[1], qf.at[1], pair_peer),
        remote(full.at[rows_of(pair_lo, 1 - c)], fin.at[layer, c], sf.at[2], qf.at[2], cross_peer),
    ]
    for copy in fcopies:
        copy.start()
    fin[layer, c] = full[rows_of(zlo, c)]

    half_way = three(split(rows_in[...]), split(full[...]))
    newrows[...] = base[...] - three(split(half_way), (other_hi[...], other_lo[...]))

    rcopy = remote(newrows.at[0:32], partner, sr.at[0], qr.at[0], core_peer)

    @pl.when(c == 0)
    def _():
        rcopy.start()

    targets = [device(x, y, z, 0), device(x, y, zpair, 0), device(x, y, zpair, 1)]
    order = [(layer, 0), (1 - layer, 0), (1 - layer, 1)]
    pcopies = [
        remote(pblock.at[a * 2 + b], pin.at[layer], sp.at[k], qp.at[layer], targets[k])
        for k, (a, b) in enumerate(order)
    ]

    @pl.when(c == 1)
    def _():
        rcopy.wait_recv()
        result = three(split(newrows[...]), split(partner[...]), (((1,), (1,)), ((), ())))
        for k in range(4):
            pblock[k] = result[16 * k : 16 * k + 16]
        pin[layer] = pblock[layer * 2 + 1]
        for copy in pcopies:
            copy.start()

    for copy in fcopies:
        copy.wait()
    for l in range(2):
        for s in range(2):
            keep_slot = jnp.where(owners[l, s] == grp, 1.0, 0.0).astype(jnp.float32)
            slots_out[l, s] = fin[l, s] * keep_slot

    @pl.when(c == 0)
    def _():
        rcopy.wait_send()
        remote(pblock.at[0], pin.at[layer], sp.at[0], qp.at[layer], core_peer).wait_recv()

    @pl.when(c == 1)
    def _():
        for copy in pcopies:
            copy.wait_send()

    remote(pblock.at[0], pin.at[1 - layer], sp.at[0], qp.at[1 - layer], core_peer).wait_recv()
    pre_out[...] = pin[...]


def body(activations, out_grads, inverse_slots, gradient, owners, counts):
    f32, bf16 = jnp.float32, jnp.bfloat16
    whole = pl.BlockSpec(memory_space=pltpu.VMEM)
    vm = lambda *shape: pltpu.VMEM(shape, f32)
    dma = lambda n: pltpu.SemaphoreType.DMA((n,))
    operands = (owners, counts, activations, out_grads, inverse_slots, gradient)
    return pl.pallas_call(
        kernel,
        out_shape=(
            jax.ShapeDtypeStruct((2, 2, 16, 512), f32),
            jax.ShapeDtypeStruct((2, 16, 32), f32),
        ),
        in_specs=[pl.BlockSpec(memory_space=pltpu.HBM)] * 6,
        out_specs=(whole, whole),
        scratch_shapes=[
            pltpu.SMEM((2, 2), jnp.int32),
            pltpu.SMEM((512,), jnp.int32),
            pltpu.VMEM((2, 2, 128, 512), bf16),
            vm(2, 2, 16, 512),
            vm(512, 512),
            vm(2, 512, 128),
            vm(2, 512, 128),
            pltpu.VMEM((2, 512, 256), bf16),
            vm(2, 4, 4, 8, 8, 128),
            vm(2, 4, 3, 4, 2, 8, 128),
            vm(2, 4, 4, 2, 8, 128),
            vm(2, 4, 3, 2, 8, 128),
            vm(2, 4, 2, 8, 128),
            vm(15, 8, 128),
            vm(8, 128),
            vm(8, 8, 128),
            vm(16, 8, 8, 128),
            vm(16, 8, 8, 128),
            vm(512, 512),
            vm(4, 2, 2, 18, 128),
            vm(3, 2, 2, 18, 128),
            vm(2, 2, 18, 128),
            vm(2, 18, 128),
            vm(2, 2, 16, 128),
            vm(15, 2, 16, 128),
            vm(4, 2, 16, 128),
            vm(4, 4, 4, 2, 16, 128),
            vm(512, 512),
            vm(64, 512),
            pltpu.VMEM((512, 512), bf16),
            pltpu.VMEM((512, 512), bf16),
            vm(64, 512),
            vm(2, 2, 128),
            vm(15, 2, 128),
            vm(2, 128),
            vm(3, 2, 128),
            vm(64, 512),
            vm(32, 512),
            vm(4, 16, 32),
            vm(2, 16, 32),
            vm(2, 2, 16, 512),
            dma(6), dma(2), dma(2), dma(24), dma(24), dma(24), dma(24), dma(15), dma(15), dma(7), dma(7),
            dma(75), dma(75),
            dma(3), dma(3), dma(1), dma(1), dma(15), dma(15), dma(60), dma(60), dma(15), dma(15), dma(3), dma(3),
            dma(3), dma(3), dma(1), dma(1), dma(3), dma(2),
            pltpu.SemaphoreType.REGULAR((2,)),
        ],
        compiler_params=pltpu.CompilerParams(
            collective_id=0, has_side_effects=True, vmem_limit_bytes=40 * 1024 * 1024
        ),
    )(*(pltpu.with_memory_space_constraint(a, pltpu.HBM) for a in operands))


def solution(mesh):
    placed = (
        P(None, ("grp", "mem"), None),
        P(None, ("grp", "mem"), None),
        P(None, None, ("grp", "mem"), None),
        P(),
        P(),
        P(),
    )
    return jax.shard_map(
        body,
        mesh=mesh,
        in_specs=placed,
        out_specs=(P(None, None, ("grp", "mem"), None), P(None, "mem", "grp")),
        check_vma=False,
    )
```
